512 devices in a mesh: rep: 64 (over y_lo, z, core), fsdp: 8 (over y_hi, x).
Axes of the slice: x: 4, y: 4 (y_hi: 2, y_lo: 2; y = y_hi * 2 + y_lo), z: 16, core: 2. Of those that a mesh axis runs over, the one named last changes fastest.
Arguments:
- weights: bfloat16 [64, 4096, 512], P('rep', 'fsdp'), may hold values from -6 to 6
- first_moment: bfloat16 [64, 4096, 512], P('rep', 'fsdp'), may hold values from -4 to 4
- second_moment: bfloat16 [64, 4096, 512], P('rep', 'fsdp'), may hold values from 0.049804688 to 1
- inputs: bfloat16 [64, 1536, 4096], P('rep', 'fsdp'), may hold values from -6 to 6
- cotangent: bfloat16 [64, 1536, 512], P('rep', 'fsdp'), may hold values from -6 to 6
- global_frag: float32 [4096, 128], P(('fsdp', 'rep')), may hold values from -6 to 6
- outer_momentum: bfloat16 [4096, 128], P(('fsdp', 'rep')), may hold values from -6 to 6
- fragment: int32 [4], replicated, may hold values from 0 to 3, each once
- inner_step: int32 [64], P('rep'), may hold values from 1 to 4
Outputs:
- new_weights: bfloat16 [64, 4096, 512], P('rep', 'fsdp')
- new_first: bfloat16 [64, 4096, 512], P('rep', 'fsdp')
- new_second: bfloat16 [64, 4096, 512], P('rep', 'fsdp')
- new_global: float32 [4096, 128], P(('fsdp', 'rep'))
- new_momentum: bfloat16 [4096, 128], P(('fsdp', 'rep'))
The draws below stay inside these ranges and needn't reach their ends.
Inputs may be any that keep to these rules, and one draw needn't show every extreme that they name: `fragment`: each of 0 to 3 once.
All inputs are finite; a program needn't handle non-finite values.
Results may differ from the reference program's by a relative error of at most 0.0065.
Values may be sent and summed in bfloat16 or wider, within the bound.
A program may use at most 64 MiB of HBM per device.

```python
import math
import jax
import jax.numpy as jnp
from jax import lax

DIN = 4096
KVH = 4
HEAD = 128
TOK_DEV = 192
DKV = 512
SEQ_TOK = 1536
REPLICAS = 64
N_FSDP = 8


def with_ends(values, stream_key, least, top_value):
    dims = values.shape
    index_at = [jax.random.randint(jax.random.fold_in(stream_key, axis), (), 0, dims[axis]) for axis in range(len(dims))]
    values = values.at[tuple(index_at)].set(least)
    longest = dims.index(max(dims))
    index_at[longest] = (index_at[longest] + 1) % dims[longest]
    return values.at[tuple(index_at)].set(top_value)


def block_scale(key, dims, pieces, smallest, top_value):
    def one(dim, blocks):
        draws = jax.random.uniform(jax.random.fold_in(jax.random.fold_in(key, 6), dim), (blocks,), jnp.float32, smallest / len(pieces), top_value / len(pieces))
        return jnp.repeat(jnp.exp(draws), dims[dim] // blocks).reshape((-1,) + (1,) * (len(dims) - dim - 1))

    loudness = one(*pieces[0])
    for cut in pieces[1:]:
        loudness = loudness * one(*cut)
    return loudness


def centred(own_key, extent, scale, bound, pieces=(), held_as=jnp.bfloat16):
    loudness = block_scale(own_key, extent, pieces, -0.22, 0.18) if pieces else 1.0
    values = jax.random.normal(own_key, extent, jnp.float32) * scale * loudness
    return jnp.minimum(jnp.maximum(values, -bound), bound).astype(held_as)


def setup_inputs(seed: int = 0) -> dict:
    arg_keys = jax.random.split(jax.random.key(seed), 10)
    return {
        "weights": centred(arg_keys[0], (REPLICAS, DIN, DKV), 1.0, 6.0, ((0, 64), (1, 8))),
        "first_moment": centred(arg_keys[1], (REPLICAS, DIN, DKV), 0.3, 4.0, ((0, 64), (1, 8))),
        "second_moment": jnp.clip(jnp.exp(math.log(1.0) - 2.9996462 * jax.random.uniform(arg_keys[2], (REPLICAS, DIN, DKV), jnp.float32) ** block_scale(arg_keys[2], (REPLICAS, DIN, DKV), ((0, 64), (1, 8)), -0.2, 0.2)), 0.049804688, 1.0).astype(jnp.bfloat16),
        "inputs": centred(arg_keys[3], (REPLICAS, SEQ_TOK, DIN), 1.0, 6.0, ((0, 64), (1, 8))),
        "cotangent": centred(arg_keys[4], (REPLICAS, SEQ_TOK, DKV), 1.0, 6.0, ((0, 64), (1, 8))),
        "global_frag": centred(arg_keys[5], (DIN, HEAD), 1.0, 6.0, ((0, 512),), jnp.float32),
        "outer_momentum": centred(arg_keys[6], (DIN, HEAD), 0.5, 6.0, ((0, 512),)),
        "fragment": jax.random.permutation(arg_keys[7], KVH).astype(jnp.int32),
        "inner_step": with_ends(jax.random.randint(arg_keys[8], (REPLICAS,), 1, 5), jax.random.fold_in(arg_keys[8], 1), 1, 4).astype(jnp.int32),
    }


beta_first = 0.9
beta_second = 0.95
rate_unit = 0.05
weight_decay = 0.1
adam_epsilon = 1e-08
norm_epsilon = 1e-06
outer_rate = 0.7
outer_beta = 0.9
mix_share = 0.5

def column_rates(fragment):
    places = jnp.arange(KVH, dtype=jnp.int32)
    matches = (fragment[:, None] == places[None, :]).astype(jnp.float32)
    positions = lax.optimization_barrier(jnp.sum(places.astype(jnp.float32)[:, None] * matches, axis=0))
    rates = rate_unit * (1.0 + positions)
    return jnp.repeat(rates, HEAD)

def key_gradient(keys, cotangent_rows):
    token_count = keys.shape[0]
    heads = keys.reshape(token_count, -1, HEAD)
    scale = lax.rsqrt(lax.optimization_barrier(jnp.mean(heads * heads, axis=-1, keepdims=True)) + norm_epsilon)
    normed = heads * scale
    upstream = cotangent_rows.astype(jnp.float32).reshape(heads.shape)
    along = lax.optimization_barrier(jnp.mean(upstream * normed, axis=-1, keepdims=True))
    return (scale * (upstream - normed * along)).reshape(token_count, -1)

def adam_update(weight_rows, first_rows, second_rows, gradient, step_value, rates):
    first_full = beta_first * first_rows.astype(jnp.float32) + (1.0 - beta_first) * gradient
    second_full = beta_second * second_rows.astype(jnp.float32) + (1.0 - beta_second) * gradient * gradient
    first_hat = first_full / (1.0 - jnp.power(beta_first, step_value))
    second_hat = second_full / (1.0 - jnp.power(beta_second, step_value))
    weight_float = weight_rows.astype(jnp.float32)
    updated = weight_float - rates[None, :] * (first_hat / (jnp.sqrt(second_hat) + adam_epsilon) + weight_decay * weight_float)
    return (updated, first_full.astype(jnp.bfloat16), second_full.astype(jnp.bfloat16))

def outer_update(global_rows, momentum_rows, average):
    momentum_full = outer_beta * momentum_rows.astype(jnp.float32) + average
    global_new = global_rows - outer_rate * (average + outer_beta * momentum_full)
    return (global_new, momentum_full.astype(jnp.bfloat16))

def mix_fragment(updated, global_new, column_start):
    own_block = lax.dynamic_slice_in_dim(updated, column_start, HEAD, 1)
    blended = mix_share * own_block + (1.0 - mix_share) * global_new
    return lax.dynamic_update_slice_in_dim(updated, blended, column_start, 1)

def reference(weights, first_moment, second_moment, inputs, cotangent, global_frag, outer_momentum, fragment, inner_step):
    column_start = (fragment[0] * HEAD).astype(jnp.int32)
    rates = column_rates(fragment)

    def replica_block(weight_rows):
        return lax.dynamic_slice_in_dim(weight_rows, column_start, HEAD, 1).astype(jnp.float32)
    average = global_frag - lax.optimization_barrier(jnp.sum(lax.map(replica_block, weights), axis=0)) / REPLICAS
    global_new, momentum_new = outer_update(global_frag, outer_momentum, average)

    def replica_step(packed):
        weight_rows, first_rows, second_rows, token_rows, cotangent_rows, step_count = packed
        step_value = step_count.astype(jnp.float32)
        keys = jnp.dot(token_rows, weight_rows, preferred_element_type=jnp.float32)
        key_grad = key_gradient(keys, cotangent_rows).astype(jnp.bfloat16)
        token_blocks = token_rows.reshape(N_FSDP, TOK_DEV, DIN).astype(jnp.float32)
        grad_blocks = key_grad.reshape(N_FSDP, TOK_DEV, -1).astype(jnp.float32)
        partial_terms = jnp.einsum('fti,ftk->fik', token_blocks, grad_blocks)
        rounded = lax.optimization_barrier(partial_terms.astype(jnp.bfloat16))
        gradient = lax.optimization_barrier(jnp.sum(rounded.astype(jnp.float32), axis=0))
        updated, first_new, second_new = adam_update(weight_rows, first_rows, second_rows, gradient, step_value, rates)
        updated = mix_fragment(updated, global_new, column_start)
        return (updated.astype(jnp.bfloat16), first_new, second_new)
    new_weights, new_first, new_second = lax.map(replica_step, (weights, first_moment, second_moment, inputs, cotangent, inner_step))
    return (new_weights, new_first, new_second, global_new, momentum_new)
```

```python
import functools
import math

import jax
import jax.numpy as jnp
from jax import lax
from jax.experimental import pallas as pl
from jax.experimental.pallas import tpu as pltpu
from jax.sharding import PartitionSpec as P

KVH = 4
HEAD = 128
NX = 4
NY = 2

beta_first = 0.9
beta_second = 0.95
rate_unit = 0.05
weight_decay = 0.1
adam_epsilon = 1e-08
norm_epsilon = 1e-06
outer_rate = 0.7
outer_beta = 0.9
mix_share = 0.5

CHUNKS = 2
MESH = pl.DeviceIdType.MESH
f32 = jnp.float32
bf16 = jnp.bfloat16


def kernel(
    n_rep,
    x_hbm, w_hbm, m_hbm, v_hbm, ct_hbm, gf_ref, om_ref, frag_ref, step_ref,
    nw_hbm, nf_hbm, ns_hbm, ng_ref, nm_ref,
    xall, xt, wall, mv, vv, ct, kown, psend, precv, kgall, gsend, grecv, gown, wout, fout, sout,
    fbuf, fcore, s1, fyl, s2, zrecv, ngall, ng2, ngf,
    lsem, xs, xr, ws, wr, rss, rsr, ags, agr, gs, gr, fs, fr, zs, zr, z2s, z2r, osem, near, far,
):
    nz = n_rep // 4
    tokens = ct.shape[0]
    tok = tokens // CHUNKS
    block = w_hbm.shape[0]
    rep = lax.axis_index("rep")
    me = lax.axis_index("fsdp")
    y, x = me // NX, lax.rem(me, NX)
    core, z, ylo = lax.rem(rep, 2), lax.rem(rep // 2, nz), rep // (2 * nz)
    others = (2, 1, 3)

    def x_peer(o):
        return (rep, y * NX + lax.rem(x + o, NX))

    def z_peer(k):
        return (ylo * 2 * nz + lax.rem(z + k, nz) * 2 + core, me)

    y_peer = (rep, (1 - y) * NX + x)
    core_peer = (rep + 1 - 2 * core, me)
    ylo_peer = ((1 - ylo) * 2 * nz + z * 2 + core, me)

    def remote(src, dst, send, recv, device):
        return pltpu.make_async_remote_copy(
            src_ref=src, dst_ref=dst, send_sem=send, recv_sem=recv,
            device_id=device, device_id_type=MESH,
        )

    def columns(h):
        return pl.ds(h * HEAD, HEAD)

    loads = [
        pltpu.make_async_copy(w_hbm, wall.at[y], lsem.at[0]),
        pltpu.make_async_copy(ct_hbm, ct, lsem.at[1]),
        pltpu.make_async_copy(m_hbm, mv, lsem.at[2]),
        pltpu.make_async_copy(v_hbm, vv, lsem.at[3]),
    ]
    for yy in range(NY):
        start = pl.multiple_of((yy * NX + x) * block, block)
        loads.append(
            pltpu.make_async_copy(
                x_hbm.at[:, pl.ds(start, block)], xall.at[yy, pl.ds(0, tokens)], lsem.at[4 + yy]
            )
        )
    for load in loads:
        load.start()

    near_z = [1, 2, nz - 2, nz - 1] if nz > 4 else []
    peers = [x_peer(o) for o in others] + [y_peer, core_peer, ylo_peer] + [z_peer(k) for k in near_z]
    barrier = pltpu.get_barrier_semaphore()
    for peer in peers:
        pl.semaphore_signal(barrier, inc=1, device_id=peer, device_id_type=MESH)
    pl.semaphore_wait(barrier, len(peers))

    w_copy = remote(w_hbm, wall.at[y], ws.at[0], wr.at[0], y_peer)
    w_copy.start()
    x_copy = {}
    for c in range(CHUNKS):
        for o in others:
            for yy in range(NY):
                start = pl.multiple_of((yy * NX + lax.rem(x + o, NX)) * block, block)
                x_copy[o, c, yy] = remote(
                    x_hbm.at[pl.ds(c * tok, tok), pl.ds(start, block)],
                    xall.at[yy, pl.ds(o * tokens + c * tok, tok)],
                    xs.at[o, c, yy], xr.at[o, c, yy], x_peer(o),
                )
                x_copy[o, c, yy].start()
    if nz > 4:
        for k in near_z:
            pl.semaphore_signal(near, inc=1, device_id=z_peer(k), device_id_type=MESH)

    chosen = [jnp.where(frag_ref[0] == h, 1.0, 0.0) for h in range(KVH)]
    loads[0].wait()
    picked = sum(chosen[h] * wall[y, :, columns(h)].astype(f32) for h in range(KVH))
    fbuf[...] = picked.reshape(fbuf.shape)
    core_copy = remote(fbuf.at[:, :, 1 - core], fcore, fs.at[0], fr.at[0], core_peer)
    core_copy.start()
    core_copy.wait_recv()
    s1[...] = fbuf[:, :, core] + fcore[...]
    ylo_copy = remote(s1.at[1 - ylo], fyl, fs.at[1], fr.at[1], ylo_peer)
    ylo_copy.start()
    if nz > 4:
        pl.semaphore_wait(near, 4)
        for k in (3, 4, nz - 4, nz - 3):
            pl.semaphore_signal(far, inc=1, device_id=z_peer(k), device_id_type=MESH)
    ylo_copy.wait_recv()
    s2[...] = s1[ylo] + fyl[...]
    if nz > 4:
        pl.semaphore_wait(far, 4)

    def z_sum(k):
        return remote(s2.at[lax.rem(z + k, nz)], zrecv.at[k], zs.at[k], zr.at[k], z_peer(k))

    def z_gather(k):
        return remote(ngall.at[z], ngall.at[z], z2s.at[k], z2r.at[k], z_peer(k))

    def each_z(act):
        if nz > 1:
            lax.fori_loop(1, nz, lambda k, carry: (act(k), carry)[1], 0)

    each_z(lambda k: z_sum(k).start())

    rs_copy, ag_copy = {}, {}

    def partial_keys(c, o):
        if o:
            for yy in range(NY):
                x_copy[o, c, yy].wait_recv()
        rows = pl.ds(o * tokens + c * tok, tok)
        for pair in range(KVH // 2):
            wide = pl.ds(pair * 2 * HEAD, 2 * HEAD)
            part = jnp.dot(xall[0, rows, :], wall[0, :, wide], preferred_element_type=f32)
            part += jnp.dot(xall[1, rows, :], wall[1, :, wide], preferred_element_type=f32)
            for i in range(2):
                h = 2 * pair + i
                own = part[:, i * HEAD:(i + 1) * HEAD]
                if o == 0:
                    kown[c, h] = own
                else:
                    psend[o, c, h] = own.astype(bf16)
                    rs_copy[o, c, h] = remote(
                        psend.at[o, c, h], precv.at[o, c, h], rss.at[o, c, h], rsr.at[o, c, h],
                        x_peer(NX - o),
                    )
                    rs_copy[o, c, h].start()

    def key_gradient(c, h):
        keys = kown[c, h]
        for o in others:
            rs_copy[o, c, h].wait_recv()
            keys += precv[o, c, h].astype(f32)
        scale = lax.rsqrt(jnp.mean(keys * keys, axis=-1, keepdims=True) + norm_epsilon)
        normed = keys * scale
        upstream = ct[pl.ds(c * tok, tok), columns(h)].astype(f32)
        along = jnp.mean(upstream * normed, axis=-1, keepdims=True)
        kgall[h, pl.ds(c * tok, tok), :] = (scale * (upstream - normed * along)).astype(bf16)
        for o in others:
            ag_copy[o, c, h] = remote(
                kgall.at[h, pl.ds(c * tok, tok)], kgall.at[h, pl.ds(o * tokens + c * tok, tok)],
                ags.at[o, c, h], agr.at[o, c, h], x_peer(o),
            )
            ag_copy[o, c, h].start()

    w_copy.wait_recv()
    for c in range(CHUNKS):
        if c == CHUNKS - 1:
            each_z(lambda k: z_sum(k).wait_recv())
            total = s2[z]
            if nz > 1:
                total += jnp.sum(zrecv[pl.ds(1, nz - 1)], axis=0)
            average = gf_ref[...] - total / n_rep
            momentum_full = outer_beta * om_ref[...].astype(f32) + average
            global_new = gf_ref[...] - outer_rate * (average + outer_beta * momentum_full)
            ng_ref[...] = global_new
            nm_ref[...] = momentum_full.astype(bf16)
            ngall[z] = global_new
            each_z(lambda k: z_gather(k).start())
        for o in others:
            partial_keys(c, o)
    loads[4].wait()
    loads[5].wait()
    loads[1].wait()
    for c in range(CHUNKS):
        partial_keys(c, 0)
    for c in range(CHUNKS):
        for h in range(KVH):
            key_gradient(c, h)
    for yy in range(NY):
        for piece in range(xall.shape[1] // 256):
            rows = pl.ds(piece * 256, 256)
            xt[yy, :, rows] = xall[yy, rows, :].T

    each_z(lambda k: z_gather(k).wait_recv())
    ylo_back = remote(ngall, ng2.at[ylo], fs.at[2], fr.at[2], ylo_peer)
    ylo_back.start()
    ng2[ylo] = ngall[...]

    g_copy = {}

    def gradient(h):
        for c in range(CHUNKS):
            for o in others:
                ag_copy[o, c, h].wait_recv()
        gsend[h] = jnp.dot(xt[1 - y], kgall[h], preferred_element_type=f32).astype(bf16)
        g_copy[h] = remote(gsend.at[h], grecv.at[h], gs.at[h], gr.at[h], y_peer)
        g_copy[h].start()
        gown[h] = jnp.dot(xt[y], kgall[h], preferred_element_type=f32)

    for h in range(KVH):
        gradient(h)
        if h == 1:
            ylo_back.wait_recv()
            core_back = remote(ng2, ngf.at[:, :, core], fs.at[3], fr.at[3], core_peer)
            core_back.start()
            ngf[:, :, core] = ng2[...]
    core_back.wait_recv()
    loads[2].wait()
    loads[3].wait()

    time = jnp.full((1, HEAD), step_ref[0].astype(f32), f32)
    first_unbias = 1.0 / (1.0 - jnp.exp(time * math.log(beta_first)))
    second_unbias = 1.0 / (1.0 - jnp.exp(time * math.log(beta_second)))
    outs = []
    for h in range(KVH):
        position = sum(jnp.where(frag_ref[j] == h, float(j), 0.0) for j in range(KVH))
        rate = rate_unit * (1.0 + position)
        g_copy[h].wait_recv()
        grad = gown[h] + grecv[h].astype(f32)
        first = beta_first * mv[:, columns(h)].astype(f32) + (1.0 - beta_first) * grad
        second = beta_second * vv[:, columns(h)].astype(f32) + (1.0 - beta_second) * grad * grad
        weight = wall[y, :, columns(h)].astype(f32)
        updated = weight - rate * (
            first * first_unbias / (jnp.sqrt(second * second_unbias) + adam_epsilon)
            + weight_decay * weight
        )
        share = (1.0 - mix_share) * chosen[h]
        updated = (1.0 - share) * updated + share * ngf[...].reshape(block, HEAD)
        wout[h] = updated.astype(bf16)
        fout[h] = first.astype(bf16)
        sout[h] = second.astype(bf16)
        for i, (buf, out) in enumerate(((wout, nw_hbm), (fout, nf_hbm), (sout, ns_hbm))):
            copy = pltpu.make_async_copy(buf.at[h], out.at[:, columns(h)], osem.at[i, h])
            copy.start()
            outs.append(copy)

    for copy in [w_copy, core_copy, ylo_copy, ylo_back, core_back, *g_copy.values()]:
        copy.wait_send()
    for copies in (x_copy, rs_copy, ag_copy):
        for copy in copies.values():
            copy.wait_send()
    each_z(lambda k: z_sum(k).wait_send())
    each_z(lambda k: z_gather(k).wait_send())
    for copy in outs:
        copy.wait()


def solution(mesh):
    n_rep = mesh.shape["rep"]
    nz = n_rep // 4

    def local(weights, first, second, inputs, cotangent, global_frag, outer_momentum, fragment, inner_step):
        block, wide = weights.shape[1:]
        tokens, din = inputs.shape[1:]
        tok = tokens // CHUNKS
        share = global_frag.shape[0]
        any_spec = pl.BlockSpec(memory_space=pl.ANY)
        vmem = pl.BlockSpec(memory_space=pltpu.VMEM)
        smem = pl.BlockSpec(memory_space=pltpu.SMEM)
        dma = pltpu.SemaphoreType.DMA
        results = pl.pallas_call(
            functools.partial(kernel, n_rep),
            out_shape=[jax.ShapeDtypeStruct((block, wide), bf16)] * 3
            + [
                jax.ShapeDtypeStruct(global_frag.shape, f32),
                jax.ShapeDtypeStruct(outer_momentum.shape, bf16),
            ],
            in_specs=[any_spec] * 5 + [vmem] * 2 + [smem] * 2,
            out_specs=[any_spec] * 3 + [vmem] * 2,
            scratch_shapes=[
                pltpu.VMEM((NY, NX * tokens, block), bf16),
                pltpu.VMEM((NY, block, NX * tokens), bf16),
                pltpu.VMEM((NY, block, wide), bf16),
                pltpu.VMEM((block, wide), bf16),
                pltpu.VMEM((block, wide), bf16),
                pltpu.VMEM((tokens, wide), bf16),
                pltpu.VMEM((CHUNKS, KVH, tok, HEAD), f32),
                pltpu.VMEM((NX, CHUNKS, KVH, tok, HEAD), bf16),
                pltpu.VMEM((NX, CHUNKS, KVH, tok, HEAD), bf16),
                pltpu.VMEM((KVH, NX * tokens, HEAD), bf16),
                pltpu.VMEM((KVH, block, HEAD), bf16),
                pltpu.VMEM((KVH, block, HEAD), bf16),
                pltpu.VMEM((KVH, block, HEAD), f32),
                pltpu.VMEM((KVH, block, HEAD), bf16),
                pltpu.VMEM((KVH, block, HEAD), bf16),
                pltpu.VMEM((KVH, block, HEAD), bf16),
                pltpu.VMEM((2, nz, 2, share, HEAD), f32),
                pltpu.VMEM((2, nz, share, HEAD), f32),
                pltpu.VMEM((2, nz, share, HEAD), f32),
                pltpu.VMEM((nz, share, HEAD), f32),
                pltpu.VMEM((nz, share, HEAD), f32),
                pltpu.VMEM((nz, share, HEAD), f32),
                pltpu.VMEM((nz, share, HEAD), f32),
                pltpu.VMEM((2, nz, share, HEAD), f32),
                pltpu.VMEM((2, nz, 2, share, HEAD), f32),
                dma((6,)),
                dma((NX, CHUNKS, NY)), dma((NX, CHUNKS, NY)),
                dma((1,)), dma((1,)),
                dma((NX, CHUNKS, KVH)), dma((NX, CHUNKS, KVH)),
                dma((NX, CHUNKS, KVH)), dma((NX, CHUNKS, KVH)),
                dma((KVH,)), dma((KVH,)),
                dma((4,)), dma((4,)),
                dma((nz,)), dma((nz,)), dma((nz,)), dma((nz,)),
                dma((3, KVH)),
                pltpu.SemaphoreType.REGULAR, pltpu.SemaphoreType.REGULAR,
            ],
            compiler_params=pltpu.CompilerParams(
                collective_id=0, has_side_effects=True, vmem_limit_bytes=48 * 2**20
            ),
        )(
            inputs[0], weights[0], first[0], second[0], cotangent[0],
            global_frag, outer_momentum, fragment, inner_step,
        )
        return (results[0][None], results[1][None], results[2][None], results[3], results[4])

    in_specs = (P("rep", "fsdp", None),) * 5 + (P(("fsdp", "rep"), None),) * 2 + (P(), P("rep"))
    out_specs = (P("rep", "fsdp", None),) * 3 + (P(("fsdp", "rep"), None),) * 2
    return jax.shard_map(local, mesh=mesh, in_specs=in_specs, out_specs=out_specs, check_vma=False)
```

```python
import functools
import math

import jax
import jax.numpy as jnp
from jax import lax
from jax.experimental import pallas as pl
from jax.experimental.pallas import tpu as pltpu
from jax.sharding import PartitionSpec as P

KVH = 4
HEAD = 128
NX = 4
NY = 2

beta_first = 0.9
beta_second = 0.95
rate_unit = 0.05
weight_decay = 0.1
adam_epsilon = 1e-08
norm_epsilon = 1e-06
outer_rate = 0.7
outer_beta = 0.9
mix_share = 0.5

PIECES = (192,)
ORDER = (
    "P00", "R00", "R01", "P01", "R02", "R03", "ZS", "XT", "K00", "K01", "K02", "K03", "G0", "G1", "YB",
    "G2", "G3", "CB", "M0", "M1", "M2", "M3", "A0", "A1", "A2", "A3",
)
MESH = pl.DeviceIdType.MESH
f32 = jnp.float32
bf16 = jnp.bfloat16


def kernel(
    n_rep,
    x_hbm, w_hbm, m_hbm, v_hbm, ct_hbm, gf_hbm, om_hbm, frag_hbm, step_hbm,
    nw_hbm, nf_hbm, ns_hbm, ng_hbm, nm_hbm,
    xall, xt, wall, mv, vv, ct, kown, psend, precv, kgall, gsend, grecv, gown, wout, fout, sout,
    gf_ref, om_ref, ng_ref, nm_ref, frag_ref, step_ref, fbuf, fcore, s1, fyl, s2, zrecv, ngall, ng2, ngf,
    lsem, xs, xr, ws, wr, rss, rsr, ags, agr, gs, gr, fs, fr, zs, zr, z2s, z2r, osem, near, near_z, mid, far,
):
    nz = n_rep // 4
    tokens = ct.shape[0]
    pieces = [(sum(PIECES[:c]), size) for c, size in enumerate(PIECES)]
    block = w_hbm.shape[0]
    rep = lax.axis_index("rep")
    me = lax.axis_index("fsdp")
    y, x = me // NX, lax.rem(me, NX)
    core, z, ylo = lax.rem(rep, 2), lax.rem(rep // 2, nz), rep // (2 * nz)
    others = (2, 1, 3)

    def x_peer(o):
        return (rep, y * NX + lax.rem(x + o, NX))

    def z_peer(k):
        return (ylo * 2 * nz + lax.rem(z + k, nz) * 2 + core, me)

    y_peer = (rep, (1 - y) * NX + x)
    core_peer = (rep + 1 - 2 * core, me)
    ylo_peer = ((1 - ylo) * 2 * nz + z * 2 + core, me)

    def remote(src, dst, send, recv, device):
        return pltpu.make_async_remote_copy(
            src_ref=src, dst_ref=dst, send_sem=send, recv_sem=recv,
            device_id=device, device_id_type=MESH,
        )

    def columns(h):
        return pl.ds(h * HEAD, HEAD)

    loads = [
        pltpu.make_async_copy(w_hbm, wall.at[y], lsem.at[0]),
        pltpu.make_async_copy(ct_hbm, ct, lsem.at[1]),
        pltpu.make_async_copy(m_hbm, mv, lsem.at[2]),
        pltpu.make_async_copy(v_hbm, vv, lsem.at[3]),
    ]
    for yy in range(NY):
        start = pl.multiple_of((yy * NX + x) * block, block)
        loads.append(
            pltpu.make_async_copy(
                x_hbm.at[:, pl.ds(start, block)], xall.at[yy, pl.ds(0, tokens)], lsem.at[4 + yy]
            )
        )
    loads += [
        pltpu.make_async_copy(frag_hbm, frag_ref, lsem.at[6]),
        pltpu.make_async_copy(step_hbm, step_ref, lsem.at[7]),
        pltpu.make_async_copy(gf_hbm, gf_ref, lsem.at[8]),
        pltpu.make_async_copy(om_hbm, om_ref, lsem.at[9]),
    ]
    for load in loads:
        load.start()

    def y_near(step):
        place = lax.rem(NY * y + ylo + step, 4)
        return (lax.rem(place, 2) * 2 * nz + z * 2 + core, place // 2 * NX + x)

    def x_send(c, o):
        first, size = pieces[c]
        for yy in range(NY):
            start = pl.multiple_of((yy * NX + lax.rem(x + o, NX)) * block, block)
            x_copy[o, c, yy] = remote(
                x_hbm.at[pl.ds(first, size), pl.ds(start, block)],
                xall.at[yy, pl.ds(o * tokens + first, size)],
                xs.at[o, c, yy], xr.at[o, c, yy], x_peer(o),
            )
            x_copy[o, c, yy].start()

    def tell(semaphore, devices):
        for device in devices:
            pl.semaphore_signal(semaphore, inc=1, device_id=device, device_id_type=MESH)

    around = [x_peer(1), x_peer(3), y_near(1), y_near(3)]
    barrier = pltpu.get_barrier_semaphore()
    tell(barrier, around + [core_peer])
    if nz > 1:
        z_near = [z_peer(1), z_peer(nz - 1)]

        @pl.when(z == 0)
        def _():
            pl.semaphore_wait(barrier, len(around) + 1)
            tell(barrier, z_near)

        @pl.when(z != 0)
        def _():
            @pl.when(z != nz - 1)
            def _():
                tell(barrier, z_near[:1])

            @pl.when(z != 1)
            def _():
                tell(barrier, z_near[1:])

            pl.semaphore_wait(barrier, len(around) + 3)

            @pl.when(z == nz - 1)
            def _():
                tell(barrier, z_near[:1])

            @pl.when(z == 1)
            def _():
                tell(barrier, z_near[1:])
    else:
        pl.semaphore_wait(barrier, len(around) + 1)
    tell(near, around)
    x_copy = {}
    x_send(0, 1)
    x_send(0, 3)
    pl.semaphore_wait(near, len(around))
    x_send(0, 2)
    w_copy = remote(w_hbm, wall.at[y], ws.at[0], wr.at[0], y_peer)
    w_copy.start()
    for c in range(1, len(pieces)):
        for o in others:
            x_send(c, o)

    loads[0].wait()
    loads[6].wait()
    chosen = [jnp.where(frag_ref[0] == h, 1.0, 0.0) for h in range(KVH)]
    picked = sum(chosen[h] * wall[y, :, columns(h)].astype(f32) for h in range(KVH))
    fbuf[...] = picked.reshape(fbuf.shape)
    core_copy = remote(fbuf.at[:, :, 1 - core], fcore, fs.at[0], fr.at[0], core_peer)
    core_copy.start()
    core_copy.wait_recv()
    s1[...] = fbuf[:, :, core] + fcore[...]
    ylo_copy = remote(s1.at[1 - ylo], fyl, fs.at[1], fr.at[1], ylo_peer)
    ylo_copy.start()
    if nz > 1:
        @pl.when(z == 0)
        def _():
            pl.semaphore_wait(barrier, 2)

        tell(near_z, z_near)
        pl.semaphore_wait(near_z, 2)
        tell(mid, [z_peer(2), z_peer(nz - 2)])
        pl.semaphore_wait(mid, 2)
        tell(far, [z_peer(k) for k in (3, 4, nz - 4, nz - 3)])
    ylo_copy.wait_recv()
    s2[...] = s1[ylo] + fyl[...]
    if nz > 1:
        pl.semaphore_wait(far, 4)

    def z_sum(k):
        return remote(s2.at[lax.rem(z + k, nz)], zrecv.at[k], zs.at[k], zr.at[k], z_peer(k))

    def z_gather(k):
        return remote(ngall.at[z], ngall.at[z], z2s.at[k], z2r.at[k], z_peer(k))

    def each_z(act):
        if nz > 1:
            lax.fori_loop(1, nz, lambda k, carry: (act(k), carry)[1], 0)

    each_z(lambda k: z_sum(k).start())

    rs_copy, ag_copy, g_copy, outs, back = {}, {}, {}, [], []
    arrived = set()

    def partial_keys(c, pair):
        first, size = pieces[c]
        wide = pl.ds(pair * 2 * HEAD, 2 * HEAD)
        for o in (1, 3, 2, 0):
            if (c, o) not in arrived:
                arrived.add((c, o))
                for yy in range(NY):
                    if o:
                        x_copy[o, c, yy].wait_recv()
                    elif c == 0:
                        loads[4 + yy].wait()
            rows = pl.ds(o * tokens + first, size)
            part = jnp.dot(xall[0, rows, :], wall[0, :, wide], preferred_element_type=f32)
            part += jnp.dot(xall[1, rows, :], wall[1, :, wide], preferred_element_type=f32)
            for i in range(2):
                own = part[:, i * HEAD:(i + 1) * HEAD]
                if o == 0:
                    kown[2 * pair + i, pl.ds(first, size)] = own
                else:
                    psend[o, 2 * pair + i, pl.ds(first, size)] = own.astype(bf16)

    def send_partial(c, h):
        first, size = pieces[c]
        for o in others:
            at = (o, h, pl.ds(first, size))
            rs_copy[o, c, h] = remote(
                psend.at[at], precv.at[at], rss.at[o, c, h], rsr.at[o, c, h], x_peer(NX - o)
            )
            rs_copy[o, c, h].start()

    def key_gradient(c, h):
        first, size = pieces[c]
        rows = pl.ds(first, size)
        keys = kown[h, rows]
        for o in others:
            rs_copy[o, c, h].wait_recv()
            keys += precv[o, h, rows].astype(f32)
        scale = lax.rsqrt(jnp.mean(keys * keys, axis=-1, keepdims=True) + norm_epsilon)
        normed = keys * scale
        upstream = ct[rows, columns(h)].astype(f32)
        along = jnp.mean(upstream * normed, axis=-1, keepdims=True)
        kgall[h, rows, :] = (scale * (upstream - normed * along)).astype(bf16)
        for o in others:
            ag_copy[o, c, h] = remote(
                kgall.at[h, rows], kgall.at[h, pl.ds(o * tokens + first, size)],
                ags.at[o, c, h], agr.at[o, c, h], x_peer(o),
            )
            ag_copy[o, c, h].start()

    def turn():
        for yy in range(NY):
            for piece in range(xall.shape[1] // 256):
                rows = pl.ds(piece * 256, 256)
                xt[yy, :, rows] = xall[yy, rows, :].T

    def send_gradient(h):
        for c in range(len(pieces)):
            for o in others:
                ag_copy[o, c, h].wait_recv()
        gsend[h] = jnp.dot(xt[1 - y], kgall[h], preferred_element_type=f32).astype(bf16)
        g_copy[h] = remote(gsend.at[h], grecv.at[h], gs.at[h], gr.at[h], y_peer)
        g_copy[h].start()

    def own_gradient(h):
        gown[h] = jnp.dot(xt[y], kgall[h], preferred_element_type=f32)

    def outer_update():
        each_z(lambda k: z_sum(k).wait_recv())
        total = s2[z]
        if nz > 1:
            total += jnp.sum(zrecv[pl.ds(1, nz - 1)], axis=0)
        loads[8].wait()
        loads[9].wait()
        average = gf_ref[...] - total / n_rep
        momentum_full = outer_beta * om_ref[...].astype(f32) + average
        global_new = gf_ref[...] - outer_rate * (average + outer_beta * momentum_full)
        ngall[z] = global_new
        each_z(lambda k: z_gather(k).start())
        ng_ref[...] = global_new
        nm_ref[...] = momentum_full.astype(bf16)
        outs.append(pltpu.make_async_copy(ng_ref, ng_hbm, lsem.at[10]))
        outs.append(pltpu.make_async_copy(nm_ref, nm_hbm, lsem.at[11]))
        for copy in outs:
            copy.start()

    def ylo_return():
        each_z(lambda k: z_gather(k).wait_recv())
        back.append(remote(ngall, ng2.at[ylo], fs.at[2], fr.at[2], ylo_peer))
        back[0].start()
        ng2[ylo] = ngall[...]

    def core_return():
        back[0].wait_recv()
        back.append(remote(ng2, ngf.at[:, :, core], fs.at[3], fr.at[3], core_peer))
        back[1].start()
        ngf[:, :, core] = ng2[...]

    def adam(h):
        if h == 0:
            back[1].wait_recv()
            loads[2].wait()
            loads[3].wait()
        time = jnp.full((1, HEAD), step_ref[0].astype(f32), f32)
        first_unbias = 1.0 / (1.0 - jnp.exp(time * math.log(beta_first)))
        second_unbias = 1.0 / (1.0 - jnp.exp(time * math.log(beta_second)))
        position = sum(jnp.where(frag_ref[j] == h, float(j), 0.0) for j in range(KVH))
        rate = rate_unit * (1.0 + position)
        g_copy[h].wait_recv()
        grad = gown[h] + grecv[h].astype(f32)
        first = beta_first * mv[:, columns(h)].astype(f32) + (1.0 - beta_first) * grad
        second = beta_second * vv[:, columns(h)].astype(f32) + (1.0 - beta_second) * grad * grad
        weight = wall[y, :, columns(h)].astype(f32)
        updated = weight - rate * (
            first * first_unbias / (jnp.sqrt(second * second_unbias) + adam_epsilon)
            + weight_decay * weight
        )
        share = (1.0 - mix_share) * chosen[h]
        updated = (1.0 - share) * updated + share * ngf[...].reshape(block, HEAD)
        wout[h] = updated.astype(bf16)
        fout[h] = first.astype(bf16)
        sout[h] = second.astype(bf16)
        for i, (buf, out) in enumerate(((wout, nw_hbm), (fout, nf_hbm), (sout, ns_hbm))):
            copy = pltpu.make_async_copy(buf.at[h], out.at[:, columns(h)], osem.at[i, h])
            copy.start()
            outs.append(copy)

    w_copy.wait_recv()
    loads[1].wait()
    loads[7].wait()
    steps = {
        "P": partial_keys, "R": send_partial, "K": key_gradient, "XT": turn, "G": send_gradient, "M": own_gradient,
        "ZS": outer_update, "YB": ylo_return, "CB": core_return, "A": adam,
    }
    for name in ORDER:
        if name in steps:
            steps[name]()
        else:
            steps[name[0]](*map(int, name[1:]))

    for copy in [w_copy, core_copy, ylo_copy, *back, *g_copy.values()]:
        copy.wait_send()
    for copies in (x_copy, rs_copy, ag_copy):
        for copy in copies.values():
            copy.wait_send()
    each_z(lambda k: z_sum(k).wait_send())
    each_z(lambda k: z_gather(k).wait_send())
    for copy in outs:
        copy.wait()


def writer(*refs):
    sources, targets, held, sems = refs[:5], refs[5:10], refs[10:15], refs[15]
    loads = [pltpu.make_async_copy(a, b, sems.at[0, i]) for i, (a, b) in enumerate(zip(sources, held))]
    stores = [pltpu.make_async_copy(a, b, sems.at[1, i]) for i, (a, b) in enumerate(zip(held, targets))]
    for load in loads:
        load.start()
    for load, store in zip(loads, stores):
        load.wait()
        store.start()
    for store in stores:
        store.wait()


def solution(mesh):
    n_rep = mesh.shape["rep"]
    nz = n_rep // 4

    def local(weights, first, second, inputs, cotangent, global_frag, outer_momentum, fragment, inner_step):
        block, wide = weights.shape[1:]
        tokens, din = inputs.shape[1:]
        share = global_frag.shape[0]
        hbm = pl.BlockSpec(memory_space=pltpu.HBM)
        dma = pltpu.SemaphoreType.DMA
        results = pl.pallas_call(
            functools.partial(kernel, n_rep),
            out_shape=[jax.ShapeDtypeStruct((block, wide), bf16)] * 3
            + [
                jax.ShapeDtypeStruct(global_frag.shape, f32),
                jax.ShapeDtypeStruct(outer_momentum.shape, bf16),
            ],
            in_specs=[hbm] * 9,
            out_specs=[hbm] * 5,
            scratch_shapes=[
                pltpu.VMEM((NY, NX * tokens, block), bf16),
                pltpu.VMEM((NY, block, NX * tokens), bf16),
                pltpu.VMEM((NY, block, wide), bf16),
                pltpu.VMEM((block, wide), bf16),
                pltpu.VMEM((block, wide), bf16),
                pltpu.VMEM((tokens, wide), bf16),
                pltpu.VMEM((KVH, tokens, HEAD), f32),
                pltpu.VMEM((NX, KVH, tokens, HEAD), bf16),
                pltpu.VMEM((NX, KVH, tokens, HEAD), bf16),
                pltpu.VMEM((KVH, NX * tokens, HEAD), bf16),
                pltpu.VMEM((KVH, block, HEAD), bf16),
                pltpu.VMEM((KVH, block, HEAD), bf16),
                pltpu.VMEM((KVH, block, HEAD), f32),
                pltpu.VMEM((KVH, block, HEAD), bf16),
                pltpu.VMEM((KVH, block, HEAD), bf16),
                pltpu.VMEM((KVH, block, HEAD), bf16),
                pltpu.VMEM(global_frag.shape, f32),
                pltpu.VMEM(outer_momentum.shape, bf16),
                pltpu.VMEM(global_frag.shape, f32),
                pltpu.VMEM(outer_momentum.shape, bf16),
                pltpu.SMEM(fragment.shape, jnp.int32),
                pltpu.SMEM(inner_step.shape, jnp.int32),
                pltpu.VMEM((2, nz, 2, share, HEAD), f32),
                pltpu.VMEM((2, nz, share, HEAD), f32),
                pltpu.VMEM((2, nz, share, HEAD), f32),
                pltpu.VMEM((nz, share, HEAD), f32),
                pltpu.VMEM((nz, share, HEAD), f32),
                pltpu.VMEM((nz, share, HEAD), f32),
                pltpu.VMEM((nz, share, HEAD), f32),
                pltpu.VMEM((2, nz, share, HEAD), f32),
                pltpu.VMEM((2, nz, 2, share, HEAD), f32),
                dma((12,)),
                dma((NX, len(PIECES), NY)), dma((NX, len(PIECES), NY)),
                dma((1,)), dma((1,)),
                dma((NX, len(PIECES), KVH)), dma((NX, len(PIECES), KVH)),
                dma((NX, len(PIECES), KVH)), dma((NX, len(PIECES), KVH)),
                dma((KVH,)), dma((KVH,)),
                dma((4,)), dma((4,)),
                dma((nz,)), dma((nz,)), dma((nz,)), dma((nz,)),
                dma((3, KVH)),
                *[pltpu.SemaphoreType.REGULAR] * 4,
            ],
            compiler_params=pltpu.CompilerParams(
                collective_id=0, has_side_effects=True, vmem_limit_bytes=60 * 2**20
            ),
        )(
            inputs[0], weights[0], first[0], second[0], cotangent[0],
            global_frag, outer_momentum, fragment, inner_step,
        )
        results = pl.pallas_call(
            writer,
            out_shape=[jax.ShapeDtypeStruct(r.shape, r.dtype) for r in results],
            in_specs=[hbm] * 5,
            out_specs=[hbm] * 5,
            scratch_shapes=[*[pltpu.VMEM(r.shape, r.dtype) for r in results], dma((2, 5))],
            compiler_params=pltpu.CompilerParams(vmem_limit_bytes=60 * 2**20),
        )(*results)
        return (results[0][None], results[1][None], results[2][None], results[3], results[4])

    in_specs = (P("rep", "fsdp", None),) * 5 + (P(("fsdp", "rep"), None),) * 2 + (P(), P("rep"))
    out_specs = (P("rep", "fsdp", None),) * 3 + (P(("fsdp", "rep"), None),) * 2
    return jax.shard_map(local, mesh=mesh, in_specs=in_specs, out_specs=out_specs, check_vma=False)
```

```python
import functools
import math

import jax
import jax.numpy as jnp
from jax import lax
from jax.experimental import pallas as pl
from jax.experimental.pallas import tpu as pltpu
from jax.sharding import PartitionSpec as P

KVH = 4
HEAD = 128
NX = 4
NY = 2

beta_first = 0.9
beta_second = 0.95
rate_unit = 0.05
weight_decay = 0.1
adam_epsilon = 1e-08
norm_epsilon = 1e-06
outer_rate = 0.7
outer_beta = 0.9
mix_share = 0.5

PIECES = (192,)
ORDER = (
    "P00", "R00", "R01", "P01", "R02", "R03", "Z0", "XT", "K00", "K01", "Z1", "K02", "K03", "G0", "YB",
    "G1", "G2", "G3", "M0", "M1", "CB", "M2", "M3", "L", "A0", "A1", "A2", "A3",
)
MESH = pl.DeviceIdType.MESH
f32 = jnp.float32
bf16 = jnp.bfloat16


def kernel(
    n_rep,
    x_hbm, w_hbm, m_hbm, v_hbm, ct_hbm, gf_hbm, om_hbm, frag_hbm, step_hbm,
    nw_hbm, nf_hbm, ns_hbm, ng_hbm, nm_hbm,
    xall, xt, wall, mv, vv, ct, kown, psend, precv, kgall, gsend, grecv, gown, wout, fout, sout,
    gf_ref, om_ref, ng_ref, nm_ref, frag_ref, step_ref, fbuf, fcore, s1, fyl, s2, zrecv, ngall, ng2, ngf,
    lsem, xs, xr, ws, wr, rss, rsr, ags, agr, gs, gr, fs, fr, zs, zr, z2s, z2r, osem, near, near_z, mid, far,
):
    nz = n_rep // 4
    tokens = ct.shape[0]
    pieces = [(sum(PIECES[:c]), size) for c, size in enumerate(PIECES)]
    block = w_hbm.shape[0]
    rep = lax.axis_index("rep")
    me = lax.axis_index("fsdp")
    y, x = me // NX, lax.rem(me, NX)
    core, z, ylo = lax.rem(rep, 2), lax.rem(rep // 2, nz), rep // (2 * nz)
    others = (2, 1, 3)

    def x_peer(o):
        return (rep, y * NX + lax.rem(x + o, NX))

    def z_peer(k):
        return (ylo * 2 * nz + lax.rem(z + k, nz) * 2 + core, me)

    y_peer = (rep, (1 - y) * NX + x)
    core_peer = (rep + 1 - 2 * core, me)
    ylo_peer = ((1 - ylo) * 2 * nz + z * 2 + core, me)

    def remote(src, dst, send, recv, device):
        return pltpu.make_async_remote_copy(
            src_ref=src, dst_ref=dst, send_sem=send, recv_sem=recv,
            device_id=device, device_id_type=MESH,
        )

    def columns(h):
        return pl.ds(h * HEAD, HEAD)

    loads = [
        pltpu.make_async_copy(w_hbm, wall.at[y], lsem.at[0]),
        pltpu.make_async_copy(ct_hbm, ct, lsem.at[1]),
        pltpu.make_async_copy(m_hbm, mv, lsem.at[2]),
        pltpu.make_async_copy(v_hbm, vv, lsem.at[3]),
    ]
    for yy in range(NY):
        start = pl.multiple_of((yy * NX + x) * block, block)
        loads.append(
            pltpu.make_async_copy(
                x_hbm.at[:, pl.ds(start, block)], xall.at[yy, pl.ds(0, tokens)], lsem.at[4 + yy]
            )
        )
    loads += [
        pltpu.make_async_copy(frag_hbm, frag_ref, lsem.at[6]),
        pltpu.make_async_copy(step_hbm, step_ref, lsem.at[7]),
        pltpu.make_async_copy(gf_hbm, gf_ref, lsem.at[8]),
        pltpu.make_async_copy(om_hbm, om_ref, lsem.at[9]),
    ]
    for load in loads:
        load.start()

    def y_near(step):
        place = lax.rem(NY * y + ylo + step, 4)
        return (lax.rem(place, 2) * 2 * nz + z * 2 + core, place // 2 * NX + x)

    def x_send(c, o):
        first, size = pieces[c]
        for yy in range(NY):
            start = pl.multiple_of((yy * NX + lax.rem(x + o, NX)) * block, block)
            x_copy[o, c, yy] = remote(
                x_hbm.at[pl.ds(first, size), pl.ds(start, block)],
                xall.at[yy, pl.ds(o * tokens + first, size)],
                xs.at[o, c, yy], xr.at[o, c, yy], x_peer(o),
            )
            x_copy[o, c, yy].start()

    def tell(semaphore, devices):
        for device in devices:
            pl.semaphore_signal(semaphore, inc=1, device_id=device, device_id_type=MESH)

    around = [x_peer(1), x_peer(3), y_near(1), y_near(3)]
    barrier = pltpu.get_barrier_semaphore()
    tell(barrier, around + [core_peer])
    if nz > 1:
        z_near = [z_peer(1), z_peer(nz - 1)]

        @pl.when(z == 0)
        def _():
            pl.semaphore_wait(barrier, len(around) + 1)
            tell(barrier, z_near)

        @pl.when(z != 0)
        def _():
            @pl.when(z != nz - 1)
            def _():
                tell(barrier, z_near[:1])

            @pl.when(z != 1)
            def _():
                tell(barrier, z_near[1:])

            pl.semaphore_wait(barrier, len(around) + 3)

            @pl.when(z == nz - 1)
            def _():
                tell(barrier, z_near[:1])

            @pl.when(z == 1)
            def _():
                tell(barrier, z_near[1:])
    else:
        pl.semaphore_wait(barrier, len(around) + 1)
    tell(near, around)
    x_copy = {}
    x_send(0, 1)
    x_send(0, 3)
    if nz > 1:
        @pl.when(z != 0)
        def _():
            tell(near_z, z_near)

    pl.semaphore_wait(near, len(around))
    x_send(0, 2)
    w_copy = remote(w_hbm, wall.at[y], ws.at[0], wr.at[0], y_peer)
    w_copy.start()
    for c in range(1, len(pieces)):
        for o in others:
            x_send(c, o)

    loads[0].wait()
    loads[6].wait()
    chosen = [jnp.where(frag_ref[0] == h, 1.0, 0.0) for h in range(KVH)]
    picked = sum(chosen[h] * wall[y, :, columns(h)].astype(f32) for h in range(KVH))
    fbuf[...] = picked.reshape(fbuf.shape)
    core_copy = remote(fbuf.at[:, :, 1 - core], fcore, fs.at[0], fr.at[0], core_peer)
    core_copy.start()
    core_copy.wait_recv()
    s1[...] = fbuf[:, :, core] + fcore[...]
    ylo_copy = remote(s1.at[1 - ylo], fyl, fs.at[1], fr.at[1], ylo_peer)
    ylo_copy.start()
    if nz > 1:
        @pl.when(z == 0)
        def _():
            pl.semaphore_wait(barrier, 2)
            tell(near_z, z_near)

        pl.semaphore_wait(near_z, 2)
        tell(mid, [z_peer(2), z_peer(nz - 2)])
        pl.semaphore_wait(mid, 2)
        tell(far, [z_peer(k) for k in (3, 4, nz - 4, nz - 3)])
    ylo_copy.wait_recv()
    s2[...] = s1[ylo] + fyl[...]
    if nz > 1:
        pl.semaphore_wait(far, 4)

    def z_sum(k):
        return remote(s2.at[lax.rem(z + k, nz)], zrecv.at[k], zs.at[k], zr.at[k], z_peer(k))

    def z_gather(k):
        return remote(ngall.at[z], ngall.at[z], z2s.at[k], z2r.at[k], z_peer(k))

    def each_z(act):
        if nz > 1:
            lax.fori_loop(1, nz, lambda k, carry: (act(k), carry)[1], 0)

    each_z(lambda k: z_sum(k).start())

    rs_copy, ag_copy, g_copy, back = {}, {}, {}, []
    outs = [
        pltpu.make_async_copy(ng_ref, ng_hbm, lsem.at[10]),
        pltpu.make_async_copy(nm_ref, nm_hbm, lsem.at[11]),
    ]
    arrived = set()

    def partial_keys(c, pair):
        first, size = pieces[c]
        wide = pl.ds(pair * 2 * HEAD, 2 * HEAD)
        for o in (1, 3, 2, 0):
            if (c, o) not in arrived:
                arrived.add((c, o))
                for yy in range(NY):
                    if o:
                        x_copy[o, c, yy].wait_recv()
                    elif c == 0:
                        loads[4 + yy].wait()
            rows = pl.ds(o * tokens + first, size)
            part = jnp.dot(xall[0, rows, :], wall[0, :, wide], preferred_element_type=f32)
            part += jnp.dot(xall[1, rows, :], wall[1, :, wide], preferred_element_type=f32)
            for i in range(2):
                own = part[:, i * HEAD:(i + 1) * HEAD]
                if o == 0:
                    kown[2 * pair + i, pl.ds(first, size)] = own
                else:
                    psend[o, 2 * pair + i, pl.ds(first, size)] = own.astype(bf16)

    def send_partial(c, h):
        first, size = pieces[c]
        for o in others:
            at = (o, h, pl.ds(first, size))
            rs_copy[o, c, h] = remote(
                psend.at[at], precv.at[at], rss.at[o, c, h], rsr.at[o, c, h], x_peer(NX - o)
            )
            rs_copy[o, c, h].start()

    def key_gradient(c, h):
        first, size = pieces[c]
        rows = pl.ds(first, size)
        keys = kown[h, rows]
        for o in others:
            rs_copy[o, c, h].wait_recv()
            keys += precv[o, h, rows].astype(f32)
        scale = lax.rsqrt(jnp.mean(keys * keys, axis=-1, keepdims=True) + norm_epsilon)
        normed = keys * scale
        upstream = ct[rows, columns(h)].astype(f32)
        along = jnp.mean(upstream * normed, axis=-1, keepdims=True)
        kgall[h, rows, :] = (scale * (upstream - normed * along)).astype(bf16)
        for o in others:
            ag_copy[o, c, h] = remote(
                kgall.at[h, rows], kgall.at[h, pl.ds(o * tokens + first, size)],
                ags.at[o, c, h], agr.at[o, c, h], x_peer(o),
            )
            ag_copy[o, c, h].start()

    def turn():
        for yy in range(NY):
            for piece in range(xall.shape[1] // 256):
                rows = pl.ds(piece * 256, 256)
                xt[yy, :, rows] = xall[yy, rows, :].T

    def send_gradient(h):
        for c in range(len(pieces)):
            for o in others:
                ag_copy[o, c, h].wait_recv()
        gsend[h] = jnp.dot(xt[1 - y], kgall[h], preferred_element_type=f32).astype(bf16)
        g_copy[h] = remote(gsend.at[h], grecv.at[h], gs.at[h], gr.at[h], y_peer)
        g_copy[h].start()

    def own_gradient(h):
        gown[h] = jnp.dot(xt[y], kgall[h], preferred_element_type=f32)

    def outer_update(first_plane):
        if nz > 1:
            pl.when(z == 0 if first_plane else z != 0)(outer_rows)
        elif first_plane:
            outer_rows()

    def outer_rows():
        each_z(lambda k: z_sum(k).wait_recv())
        total = s2[z]
        if nz > 1:
            total += jnp.sum(zrecv[pl.ds(1, nz - 1)], axis=0)
        loads[8].wait()
        loads[9].wait()
        average = gf_ref[...] - total / n_rep
        momentum_full = outer_beta * om_ref[...].astype(f32) + average
        global_new = gf_ref[...] - outer_rate * (average + outer_beta * momentum_full)
        ngall[z] = global_new
        each_z(lambda k: z_gather(k).start())
        ng_ref[...] = global_new
        nm_ref[...] = momentum_full.astype(bf16)
        for copy in outs:
            copy.start()

    def ylo_return():
        each_z(lambda k: z_gather(k).wait_recv())
        back.append(remote(ngall, ng2.at[ylo], fs.at[2], fr.at[2], ylo_peer))
        back[0].start()
        ng2[ylo] = ngall[...]

    def core_return():
        back[0].wait_recv()
        back.append(remote(ng2, ngf.at[:, :, core], fs.at[3], fr.at[3], core_peer))
        back[1].start()
        ngf[:, :, core] = ng2[...]

    def all_left():
        for copy in [w_copy, core_copy, ylo_copy, back[0]]:
            copy.wait_send()
        for copies in (x_copy, rs_copy, ag_copy):
            for copy in copies.values():
                copy.wait_send()
        each_z(lambda k: z_sum(k).wait_send())
        each_z(lambda k: z_gather(k).wait_send())

    def adam(h):
        if h == 0:
            back[1].wait_recv()
            loads[2].wait()
            loads[3].wait()
        time = jnp.full((1, HEAD), step_ref[0].astype(f32), f32)
        first_unbias = 1.0 / (1.0 - jnp.exp(time * math.log(beta_first)))
        second_unbias = 1.0 / (1.0 - jnp.exp(time * math.log(beta_second)))
        position = sum(jnp.where(frag_ref[j] == h, float(j), 0.0) for j in range(KVH))
        rate = rate_unit * (1.0 + position)
        g_copy[h].wait_recv()
        grad = gown[h] + grecv[h].astype(f32)
        first = beta_first * mv[:, columns(h)].astype(f32) + (1.0 - beta_first) * grad
        second = beta_second * vv[:, columns(h)].astype(f32) + (1.0 - beta_second) * grad * grad
        weight = wall[y, :, columns(h)].astype(f32)
        updated = weight - rate * (
            first * first_unbias / (jnp.sqrt(second * second_unbias) + adam_epsilon)
            + weight_decay * weight
        )
        share = (1.0 - mix_share) * chosen[h]
        updated = (1.0 - share) * updated + share * ngf[...].reshape(block, HEAD)
        wout[h] = updated.astype(bf16)
        fout[h] = first.astype(bf16)
        sout[h] = second.astype(bf16)
        for i, (buf, out) in enumerate(((wout, nw_hbm), (fout, nf_hbm), (sout, ns_hbm))):
            copy = pltpu.make_async_copy(buf.at[h], out.at[:, columns(h)], osem.at[i, h])
            copy.start()
            outs.append(copy)

    w_copy.wait_recv()
    loads[1].wait()
    loads[7].wait()
    steps = {
        "P": partial_keys, "R": send_partial, "K": key_gradient, "XT": turn, "G": send_gradient, "M": own_gradient,
        "Z": outer_update, "YB": ylo_return, "CB": core_return, "L": all_left, "A": adam,
    }
    for name in ORDER:
        if name in steps:
            steps[name]()
        else:
            steps[name[0]](*map(int, name[1:]))

    for copy in [back[1], *g_copy.values()]:
        copy.wait_send()
    for copy in outs:
        copy.wait()


def writer(*refs):
    sources, targets, held, sems = refs[:5], refs[5:10], refs[10:15], refs[15]
    loads = [pltpu.make_async_copy(a, b, sems.at[0, i]) for i, (a, b) in enumerate(zip(sources, held))]
    stores = [pltpu.make_async_copy(a, b, sems.at[1, i]) for i, (a, b) in enumerate(zip(held, targets))]
    for load in loads:
        load.start()
    for load, store in zip(loads, stores):
        load.wait()
        store.start()
    for store in stores:
        store.wait()


def solution(mesh):
    n_rep = mesh.shape["rep"]
    nz = n_rep // 4

    def local(weights, first, second, inputs, cotangent, global_frag, outer_momentum, fragment, inner_step):
        block, wide = weights.shape[1:]
        tokens, din = inputs.shape[1:]
        share = global_frag.shape[0]
        hbm = pl.BlockSpec(memory_space=pltpu.HBM)
        dma = pltpu.SemaphoreType.DMA
        results = pl.pallas_call(
            functools.partial(kernel, n_rep),
            out_shape=[jax.ShapeDtypeStruct((block, wide), bf16)] * 3
            + [
                jax.ShapeDtypeStruct(global_frag.shape, f32),
                jax.ShapeDtypeStruct(outer_momentum.shape, bf16),
            ],
            in_specs=[hbm] * 9,
            out_specs=[hbm] * 5,
            scratch_shapes=[
                pltpu.VMEM((NY, NX * tokens, block), bf16),
                pltpu.VMEM((NY, block, NX * tokens), bf16),
                pltpu.VMEM((NY, block, wide), bf16),
                pltpu.VMEM((block, wide), bf16),
                pltpu.VMEM((block, wide), bf16),
                pltpu.VMEM((tokens, wide), bf16),
                pltpu.VMEM((KVH, tokens, HEAD), f32),
                pltpu.VMEM((NX, KVH, tokens, HEAD), bf16),
                pltpu.VMEM((NX, KVH, tokens, HEAD), bf16),
                pltpu.VMEM((KVH, NX * tokens, HEAD), bf16),
                pltpu.VMEM((KVH, block, HEAD), bf16),
                pltpu.VMEM((KVH, block, HEAD), bf16),
                pltpu.VMEM((KVH, block, HEAD), f32),
                pltpu.VMEM((KVH, block, HEAD), bf16),
                pltpu.VMEM((KVH, block, HEAD), bf16),
                pltpu.VMEM((KVH, block, HEAD), bf16),
                pltpu.VMEM(global_frag.shape, f32),
                pltpu.VMEM(outer_momentum.shape, bf16),
                pltpu.VMEM(global_frag.shape, f32),
                pltpu.VMEM(outer_momentum.shape, bf16),
                pltpu.SMEM(fragment.shape, jnp.int32),
                pltpu.SMEM(inner_step.shape, jnp.int32),
                pltpu.VMEM((2, nz, 2, share, HEAD), f32),
                pltpu.VMEM((2, nz, share, HEAD), f32),
                pltpu.VMEM((2, nz, share, HEAD), f32),
                pltpu.VMEM((nz, share, HEAD), f32),
                pltpu.VMEM((nz, share, HEAD), f32),
                pltpu.VMEM((nz, share, HEAD), f32),
                pltpu.VMEM((nz, share, HEAD), f32),
                pltpu.VMEM((2, nz, share, HEAD), f32),
                pltpu.VMEM((2, nz, 2, share, HEAD), f32),
                dma((12,)),
                dma((NX, len(PIECES), NY)), dma((NX, len(PIECES), NY)),
                dma((1,)), dma((1,)),
                dma((NX, len(PIECES), KVH)), dma((NX, len(PIECES), KVH)),
                dma((NX, len(PIECES), KVH)), dma((NX, len(PIECES), KVH)),
                dma((KVH,)), dma((KVH,)),
                dma((4,)), dma((4,)),
                dma((nz,)), dma((nz,)), dma((nz,)), dma((nz,)),
                dma((3, KVH)),
                *[pltpu.SemaphoreType.REGULAR] * 4,
            ],
            compiler_params=pltpu.CompilerParams(
                collective_id=0, has_side_effects=True, vmem_limit_bytes=60 * 2**20
            ),
        )(
            inputs[0], weights[0], first[0], second[0], cotangent[0],
            global_frag, outer_momentum, fragment, inner_step,
        )
        results = pl.pallas_call(
            writer,
            out_shape=[jax.ShapeDtypeStruct(r.shape, r.dtype) for r in results],
            in_specs=[hbm] * 5,
            out_specs=[hbm] * 5,
            scratch_shapes=[*[pltpu.VMEM(r.shape, r.dtype) for r in results], dma((2, 5))],
            compiler_params=pltpu.CompilerParams(vmem_limit_bytes=60 * 2**20),
        )(*results)
        return (results[0][None], results[1][None], results[2][None], results[3], results[4])

    in_specs = (P("rep", "fsdp", None),) * 5 + (P(("fsdp", "rep"), None),) * 2 + (P(), P("rep"))
    out_specs = (P("rep", "fsdp", None),) * 3 + (P(("fsdp", "rep"), None),) * 2
    return jax.shard_map(local, mesh=mesh, in_specs=in_specs, out_specs=out_specs, check_vma=False)
```

```python
import functools
import math

import jax
import jax.numpy as jnp
from jax import lax
from jax.experimental import pallas as pl
from jax.experimental.pallas import tpu as pltpu
from jax.sharding import PartitionSpec as P

KVH = 4
HEAD = 128
NX = 4
NY = 2

beta_first = 0.9
beta_second = 0.95
rate_unit = 0.05
weight_decay = 0.1
adam_epsilon = 1e-08
norm_epsilon = 1e-06
outer_rate = 0.7
outer_beta = 0.9
mix_share = 0.5

PIECES = (192,)
ORDER = (
    "P00", "R00", "T1", "P01", "T2", "T3", "Z0", "XT", "B0", "K00", "F1", "F2", "F3", "K01", "Z1", "K02",
    "K03", "B1", "G0", "G1", "G2", "G3", "M0", "M1", "CB", "M2", "M3", "L", "A0", "A1", "A2", "A3",
)
MESH = pl.DeviceIdType.MESH
f32 = jnp.float32
bf16 = jnp.bfloat16


def kernel(
    n_rep,
    x_hbm, w_hbm, m_hbm, v_hbm, ct_hbm, gf_hbm, om_hbm, frag_hbm, step_hbm,
    nw_hbm, nf_hbm, ns_hbm, ng_hbm, nm_hbm,
    xall, xt, wall, mv, vv, ct, kown, psend, precv, kgall, gsend, grecv, gown, wout, fout, sout,
    gf_ref, om_ref, ng_ref, nm_ref, frag_ref, step_ref, fbuf, fcore, s1, fyl, s2, zrecv, ngall, ngf,
    lsem, xs, xr, ws, wr, rss, rsr, ags, agr, gs, gr, fs, fr, zs, zr, z2s, z2r, osem, near, near_z, mid, far, held, hs, hr,
):
    nz = n_rep // 4
    tokens = ct.shape[0]
    pieces = [(sum(PIECES[:c]), size) for c, size in enumerate(PIECES)]
    block = w_hbm.shape[0]
    rep = lax.axis_index("rep")
    me = lax.axis_index("fsdp")
    y, x = me // NX, lax.rem(me, NX)
    core, z, ylo = lax.rem(rep, 2), lax.rem(rep // 2, nz), rep // (2 * nz)
    others = (2, 1, 3)

    def x_peer(o):
        return (rep, y * NX + lax.rem(x + o, NX))

    def z_peer(k):
        return (ylo * 2 * nz + lax.rem(z + k, nz) * 2 + core, me)

    y_peer = (rep, (1 - y) * NX + x)
    core_peer = (rep + 1 - 2 * core, me)
    ylo_peer = ((1 - ylo) * 2 * nz + z * 2 + core, me)

    def remote(src, dst, send, recv, device):
        return pltpu.make_async_remote_copy(
            src_ref=src, dst_ref=dst, send_sem=send, recv_sem=recv,
            device_id=device, device_id_type=MESH,
        )

    def columns(h):
        return pl.ds(h * HEAD, HEAD)

    loads = [
        pltpu.make_async_copy(w_hbm, wall.at[y], lsem.at[0]),
        pltpu.make_async_copy(ct_hbm, ct, lsem.at[1]),
        pltpu.make_async_copy(m_hbm, mv, lsem.at[2]),
        pltpu.make_async_copy(v_hbm, vv, lsem.at[3]),
    ]
    for yy in range(NY):
        start = pl.multiple_of((yy * NX + x) * block, block)
        loads.append(
            pltpu.make_async_copy(
                x_hbm.at[:, pl.ds(start, block)], xall.at[yy, pl.ds(0, tokens)], lsem.at[4 + yy]
            )
        )
    loads += [
        pltpu.make_async_copy(frag_hbm, frag_ref, lsem.at[6]),
        pltpu.make_async_copy(step_hbm, step_ref, lsem.at[7]),
        pltpu.make_async_copy(gf_hbm, gf_ref, lsem.at[8]),
        pltpu.make_async_copy(om_hbm, om_ref, lsem.at[9]),
    ]
    for load in loads:
        load.start()

    def y_near(step):
        place = lax.rem(NY * y + ylo + step, 4)
        return (lax.rem(place, 2) * 2 * nz + z * 2 + core, place // 2 * NX + x)

    def x_send(c, o):
        first, size = pieces[c]
        for yy in range(NY):
            start = pl.multiple_of((yy * NX + lax.rem(x + o, NX)) * block, block)
            x_copy[o, c, yy] = remote(
                x_hbm.at[pl.ds(first, size), pl.ds(start, block)],
                xall.at[yy, pl.ds(o * tokens + first, size)],
                xs.at[o, c, yy], xr.at[o, c, yy], x_peer(o),
            )
            x_copy[o, c, yy].start()

    def tell(semaphore, devices):
        for device in devices:
            pl.semaphore_signal(semaphore, inc=1, device_id=device, device_id_type=MESH)

    around = [x_peer(1), x_peer(3), y_near(1), y_near(3)]
    barrier = pltpu.get_barrier_semaphore()
    tell(barrier, around + [core_peer])
    if nz > 1:
        z_near = [z_peer(1), z_peer(nz - 1)]

        @pl.when(z == 0)
        def _():
            pl.semaphore_wait(barrier, len(around) + 1)
            tell(barrier, z_near)

        @pl.when(z != 0)
        def _():
            @pl.when(z != nz - 1)
            def _():
                tell(barrier, z_near[:1])

            @pl.when(z != 1)
            def _():
                tell(barrier, z_near[1:])

            pl.semaphore_wait(barrier, len(around) + 3)

            @pl.when(z == nz - 1)
            def _():
                tell(barrier, z_near[:1])

            @pl.when(z == 1)
            def _():
                tell(barrier, z_near[1:])
    else:
        pl.semaphore_wait(barrier, len(around) + 1)
    tell(near, around)
    x_copy = {}
    x_send(0, 1)
    x_send(0, 3)
    if nz > 1:
        @pl.when(z != 0)
        def _():
            tell(near_z, z_near)

    pl.semaphore_wait(near, len(around))
    x_send(0, 2)
    w_copy = remote(w_hbm, wall.at[y], ws.at[0], wr.at[0], y_peer)
    w_copy.start()
    for c in range(1, len(pieces)):
        for o in others:
            x_send(c, o)

    loads[0].wait()
    loads[6].wait()
    chosen = [jnp.where(frag_ref[0] == h, 1.0, 0.0) for h in range(KVH)]
    picked = sum(chosen[h] * wall[y, :, columns(h)].astype(f32) for h in range(KVH))
    fbuf[...] = picked.reshape(fbuf.shape)
    core_copy = remote(fbuf.at[:, :, 1 - core], fcore, fs.at[0], fr.at[0], core_peer)
    core_copy.start()
    core_copy.wait_recv()
    s1[...] = fbuf[:, :, core] + fcore[...]
    ylo_copy = remote(s1.at[1 - ylo], fyl, fs.at[1], fr.at[1], ylo_peer)
    ylo_copy.start()
    if nz > 1:
        @pl.when(z == 0)
        def _():
            pl.semaphore_wait(barrier, 2)
            tell(near_z, z_near)

        pl.semaphore_wait(near_z, 2)
        tell(mid, [z_peer(2), z_peer(nz - 2)])
        pl.semaphore_wait(mid, 2)
        tell(far, [z_peer(k) for k in (3, 4, nz - 4, nz - 3)])
    ylo_copy.wait_recv()
    s2[...] = s1[ylo] + fyl[...]
    if nz > 1:
        pl.semaphore_wait(far, 4)

    def z_sum(k):
        return remote(s2.at[lax.rem(z + k, nz)], zrecv.at[k], zs.at[k], zr.at[k], z_peer(k))

    def z_gather(k):
        return remote(ngall.at[z], ngall.at[z], z2s.at[k], z2r.at[k], z_peer(k))

    def each_z(act):
        if nz > 1:
            lax.fori_loop(1, nz, lambda k, carry: (act(k), carry)[1], 0)

    each_z(lambda k: z_sum(k).start())

    rs_copy, ag_copy, g_copy = {}, {}, {}
    ylo_back = remote(ngall.at[z, ylo], ngall.at[z, ylo], fs.at[2], fr.at[2], ylo_peer)
    core_back = remote(ngall, ngf.at[:, :, core], fs.at[3], fr.at[3], core_peer)
    outs = [
        pltpu.make_async_copy(ng_ref, ng_hbm, lsem.at[10]),
        pltpu.make_async_copy(nm_ref, nm_hbm, lsem.at[11]),
    ]
    arrived = set()

    def partial_keys(c, pair):
        first, size = pieces[c]
        wide = pl.ds(pair * 2 * HEAD, 2 * HEAD)
        for o in (1, 3, 2, 0):
            if (c, o) not in arrived:
                arrived.add((c, o))
                for yy in range(NY):
                    if o:
                        x_copy[o, c, yy].wait_recv()
                    elif c == 0:
                        loads[4 + yy].wait()
            rows = pl.ds(o * tokens + first, size)
            part = jnp.dot(xall[0, rows, :], wall[0, :, wide], preferred_element_type=f32)
            part += jnp.dot(xall[1, rows, :], wall[1, :, wide], preferred_element_type=f32)
            for i in range(2):
                own = part[:, i * HEAD:(i + 1) * HEAD]
                if o == 0:
                    kown[2 * pair + i, pl.ds(first, size)] = own
                else:
                    psend[o, 2 * pair + i, pl.ds(first, size)] = own.astype(bf16)

    def send_partial(c, h):
        first, size = pieces[c]
        for o in others:
            at = (o, h, pl.ds(first, size))
            rs_copy[o, c, h] = remote(
                psend.at[at], precv.at[at], rss.at[o, c, h], rsr.at[o, c, h], x_peer(NX - o)
            )
            rs_copy[o, c, h].start()

    half = tokens // 2
    upper, lower = pl.ds(0, half), pl.ds(half, half)

    def relay_partial(h):
        for i, (o, rows) in enumerate(((1, upper), (3, lower))):
            relayed[i, h] = remote(
                psend.at[2, h, rows], held.at[i, h], hs.at[i, h], hr.at[i, h], x_peer(o)
            )
            relayed[i, h].start()
        for o, rows in ((3, lower), (1, upper)):
            rs_copy[o, 0, h] = remote(
                psend.at[o, h, rows], precv.at[o, h, rows], rss.at[o, 0, h], rsr.at[o, 0, h], x_peer(NX - o)
            )
            rs_copy[o, 0, h].start()

    def relay_sum(h):
        for i, (o, rows) in enumerate(((3, upper), (1, lower))):
            relayed[i, h].wait_recv()
            psend[o, h, rows] = (psend[o, h, rows].astype(f32) + held[i, h].astype(f32)).astype(bf16)
            relayed[2 + i, h] = remote(
                psend.at[o, h, rows], precv.at[o, h, rows], hs.at[2 + i, h], hr.at[2 + i, h], x_peer(NX - o)
            )
            relayed[2 + i, h].start()

    relayed = {}

    def key_gradient(c, h):
        first, size = pieces[c]
        rows = pl.ds(first, size)
        keys = kown[h, rows]
        for o in others:
            if (o, c, h) in rs_copy:
                rs_copy[o, c, h].wait_recv()
        if (2, h) in relayed:
            relayed[2, h].wait_recv()
            relayed[3, h].wait_recv()
        for o in others:
            if (o, c, h) in rs_copy:
                keys += precv[o, h, rows].astype(f32)
        scale = lax.rsqrt(jnp.mean(keys * keys, axis=-1, keepdims=True) + norm_epsilon)
        normed = keys * scale
        upstream = ct[rows, columns(h)].astype(f32)
        along = jnp.mean(upstream * normed, axis=-1, keepdims=True)
        kgall[h, rows, :] = (scale * (upstream - normed * along)).astype(bf16)
        for o in others:
            ag_copy[o, c, h] = remote(
                kgall.at[h, rows], kgall.at[h, pl.ds(o * tokens + first, size)],
                ags.at[o, c, h], agr.at[o, c, h], x_peer(o),
            )
            ag_copy[o, c, h].start()

    def turn():
        for yy in range(NY):
            for piece in range(xall.shape[1] // 256):
                rows = pl.ds(piece * 256, 256)
                xt[yy, :, rows] = xall[yy, rows, :].T

    def send_gradient(h):
        for c in range(len(pieces)):
            for o in others:
                ag_copy[o, c, h].wait_recv()
        gsend[h] = jnp.dot(xt[1 - y], kgall[h], preferred_element_type=f32).astype(bf16)
        g_copy[h] = remote(gsend.at[h], grecv.at[h], gs.at[h], gr.at[h], y_peer)
        g_copy[h].start()

    def own_gradient(h):
        gown[h] = jnp.dot(xt[y], kgall[h], preferred_element_type=f32)

    def outer_update(first_plane):
        if nz > 1:
            pl.when(z == 0 if first_plane else z != 0)(outer_rows)
        elif first_plane:
            outer_rows()

    def outer_rows():
        each_z(lambda k: z_sum(k).wait_recv())
        total = s2[z]
        if nz > 1:
            total += jnp.sum(zrecv[pl.ds(1, nz - 1)], axis=0)
        loads[8].wait()
        loads[9].wait()
        average = gf_ref[...] - total / n_rep
        momentum_full = outer_beta * om_ref[...].astype(f32) + average
        global_new = gf_ref[...] - outer_rate * (average + outer_beta * momentum_full)
        ngall[z, ylo] = global_new
        ylo_back.start()
        ng_ref[...] = global_new
        nm_ref[...] = momentum_full.astype(bf16)
        for copy in outs:
            copy.start()

    def gather_rows(first_plane):
        def start():
            ylo_back.wait_recv()
            each_z(lambda k: z_gather(k).start())

        if nz > 1:
            pl.when(z == 0 if first_plane else z != 0)(start)
        elif first_plane:
            start()

    def core_return():
        each_z(lambda k: z_gather(k).wait_recv())
        core_back.start()
        ngf[:, :, core] = ngall[...]

    def all_left():
        for copy in [w_copy, core_copy, ylo_copy, ylo_back]:
            copy.wait_send()
        for copies in (x_copy, rs_copy, ag_copy, relayed):
            for copy in copies.values():
                copy.wait_send()
        each_z(lambda k: z_sum(k).wait_send())
        each_z(lambda k: z_gather(k).wait_send())

    def adam(h):
        if h == 0:
            core_back.wait_recv()
            loads[2].wait()
            loads[3].wait()
        time = jnp.full((1, HEAD), step_ref[0].astype(f32), f32)
        first_unbias = 1.0 / (1.0 - jnp.exp(time * math.log(beta_first)))
        second_unbias = 1.0 / (1.0 - jnp.exp(time * math.log(beta_second)))
        position = sum(jnp.where(frag_ref[j] == h, float(j), 0.0) for j in range(KVH))
        rate = rate_unit * (1.0 + position)
        g_copy[h].wait_recv()
        grad = gown[h] + grecv[h].astype(f32)
        first = beta_first * mv[:, columns(h)].astype(f32) + (1.0 - beta_first) * grad
        second = beta_second * vv[:, columns(h)].astype(f32) + (1.0 - beta_second) * grad * grad
        weight = wall[y, :, columns(h)].astype(f32)
        updated = weight - rate * (
            first * first_unbias / (jnp.sqrt(second * second_unbias) + adam_epsilon)
            + weight_decay * weight
        )
        share = (1.0 - mix_share) * chosen[h]
        mixed = jnp.concatenate([ngf[:, i].reshape(block // 2, HEAD) for i in range(2)], axis=0)
        updated = (1.0 - share) * updated + share * mixed
        wout[h] = updated.astype(bf16)
        fout[h] = first.astype(bf16)
        sout[h] = second.astype(bf16)
        for i, (buf, out) in enumerate(((wout, nw_hbm), (fout, nf_hbm), (sout, ns_hbm))):
            copy = pltpu.make_async_copy(buf.at[h], out.at[:, columns(h)], osem.at[i, h])
            copy.start()
            outs.append(copy)

    w_copy.wait_recv()
    loads[1].wait()
    loads[7].wait()
    steps = {
        "P": partial_keys, "R": send_partial, "K": key_gradient, "XT": turn, "G": send_gradient, "M": own_gradient,
        "Z": outer_update, "B": gather_rows, "T": relay_partial, "F": relay_sum, "CB": core_return, "L": all_left, "A": adam,
    }
    for name in ORDER:
        if name in steps:
            steps[name]()
        else:
            steps[name[0]](*map(int, name[1:]))

    for copy in [core_back, *g_copy.values()]:
        copy.wait_send()
    for copy in outs:
        copy.wait()


def writer(*refs):
    sources, targets, held, sems = refs[:5], refs[5:10], refs[10:15], refs[15]
    loads = [pltpu.make_async_copy(a, b, sems.at[0, i]) for i, (a, b) in enumerate(zip(sources, held))]
    stores = [pltpu.make_async_copy(a, b, sems.at[1, i]) for i, (a, b) in enumerate(zip(held, targets))]
    for load in loads:
        load.start()
    for load, store in zip(loads, stores):
        load.wait()
        store.start()
    for store in stores:
        store.wait()


def solution(mesh):
    n_rep = mesh.shape["rep"]
    nz = n_rep // 4

    def local(weights, first, second, inputs, cotangent, global_frag, outer_momentum, fragment, inner_step):
        block, wide = weights.shape[1:]
        tokens, din = inputs.shape[1:]
        share = global_frag.shape[0]
        hbm = pl.BlockSpec(memory_space=pltpu.HBM)
        dma = pltpu.SemaphoreType.DMA
        results = pl.pallas_call(
            functools.partial(kernel, n_rep),
            out_shape=[jax.ShapeDtypeStruct((block, wide), bf16)] * 3
            + [
                jax.ShapeDtypeStruct(global_frag.shape, f32),
                jax.ShapeDtypeStruct(outer_momentum.shape, bf16),
            ],
            in_specs=[hbm] * 9,
            out_specs=[hbm] * 5,
            scratch_shapes=[
                pltpu.VMEM((NY, NX * tokens, block), bf16),
                pltpu.VMEM((NY, block, NX * tokens), bf16),
                pltpu.VMEM((NY, block, wide), bf16),
                pltpu.VMEM((block, wide), bf16),
                pltpu.VMEM((block, wide), bf16),
                pltpu.VMEM((tokens, wide), bf16),
                pltpu.VMEM((KVH, tokens, HEAD), f32),
                pltpu.VMEM((NX, KVH, tokens, HEAD), bf16),
                pltpu.VMEM((NX, KVH, tokens, HEAD), bf16),
                pltpu.VMEM((KVH, NX * tokens, HEAD), bf16),
                pltpu.VMEM((KVH, block, HEAD), bf16),
                pltpu.VMEM((KVH, block, HEAD), bf16),
                pltpu.VMEM((KVH, block, HEAD), f32),
                pltpu.VMEM((KVH, block, HEAD), bf16),
                pltpu.VMEM((KVH, block, HEAD), bf16),
                pltpu.VMEM((KVH, block, HEAD), bf16),
                pltpu.VMEM(global_frag.shape, f32),
                pltpu.VMEM(outer_momentum.shape, bf16),
                pltpu.VMEM(global_frag.shape, f32),
                pltpu.VMEM(outer_momentum.shape, bf16),
                pltpu.SMEM(fragment.shape, jnp.int32),
                pltpu.SMEM(inner_step.shape, jnp.int32),
                pltpu.VMEM((2, nz, 2, share, HEAD), f32),
                pltpu.VMEM((2, nz, share, HEAD), f32),
                pltpu.VMEM((2, nz, share, HEAD), f32),
                pltpu.VMEM((nz, share, HEAD), f32),
                pltpu.VMEM((nz, share, HEAD), f32),
                pltpu.VMEM((nz, share, HEAD), f32),
                pltpu.VMEM((nz, 2, share, HEAD), f32),
                pltpu.VMEM((nz, 2, 2, share, HEAD), f32),
                dma((12,)),
                dma((NX, len(PIECES), NY)), dma((NX, len(PIECES), NY)),
                dma((1,)), dma((1,)),
                dma((NX, len(PIECES), KVH)), dma((NX, len(PIECES), KVH)),
                dma((NX, len(PIECES), KVH)), dma((NX, len(PIECES), KVH)),
                dma((KVH,)), dma((KVH,)),
                dma((4,)), dma((4,)),
                dma((nz,)), dma((nz,)), dma((nz,)), dma((nz,)),
                dma((3, KVH)),
                *[pltpu.SemaphoreType.REGULAR] * 4,
                pltpu.VMEM((2, KVH, tokens // 2, HEAD), bf16),
                dma((4, KVH)), dma((4, KVH)),
            ],
            compiler_params=pltpu.CompilerParams(
                collective_id=0, has_side_effects=True, vmem_limit_bytes=60 * 2**20
            ),
        )(
            inputs[0], weights[0], first[0], second[0], cotangent[0],
            global_frag, outer_momentum, fragment, inner_step,
        )
        results = pl.pallas_call(
            writer,
            out_shape=[jax.ShapeDtypeStruct(r.shape, r.dtype) for r in results],
            in_specs=[hbm] * 5,
            out_specs=[hbm] * 5,
            scratch_shapes=[*[pltpu.VMEM(r.shape, r.dtype) for r in results], dma((2, 5))],
            compiler_params=pltpu.CompilerParams(vmem_limit_bytes=60 * 2**20),
        )(*results)
        return (results[0][None], results[1][None], results[2][None], results[3], results[4])

    in_specs = (P("rep", "fsdp", None),) * 5 + (P(("fsdp", "rep"), None),) * 2 + (P(), P("rep"))
    out_specs = (P("rep", "fsdp", None),) * 3 + (P(("fsdp", "rep"), None),) * 2
    return jax.shard_map(local, mesh=mesh, in_specs=in_specs, out_specs=out_specs, check_vma=False)
```

```python
import functools
import math

import jax
import jax.numpy as jnp
from jax import lax
from jax.experimental import pallas as pl
from jax.experimental.pallas import tpu as pltpu
from jax.sharding import PartitionSpec as P

KVH = 4
HEAD = 128
NX = 4
NY = 2

beta_first = 0.9
beta_second = 0.95
rate_unit = 0.05
weight_decay = 0.1
adam_epsilon = 1e-08
norm_epsilon = 1e-06
outer_rate = 0.7
outer_beta = 0.9
mix_share = 0.5

PIECES = (192,)
ORDER = (
    "P00", "R00", "T1", "P01", "T2", "T3", "Z0", "XT", "B0", "K00", "F1", "F2", "F3", "K01", "Z1", "K02",
    "K03", "B1", "G0", "G1", "G2", "G3", "M0", "M1", "CB", "M2", "M3", "L", "A0", "A1", "A2", "A3",
)
MESH = pl.DeviceIdType.MESH
f32 = jnp.float32
bf16 = jnp.bfloat16


def kernel(
    n_rep,
    x_hbm, w_hbm, m_hbm, v_hbm, ct_hbm, gf_hbm, om_hbm, frag_hbm, step_hbm,
    nw_hbm, nf_hbm, ns_hbm, ng_hbm, nm_hbm,
    xall, xt, wall, mv, vv, ct, kown, psend, precv, kgall, gsend, grecv, gown, wout, fout, sout,
    gf_ref, om_ref, ng_ref, nm_ref, frag_ref, step_ref, fbuf, fcore, s1, fyl, s2, zrecv, ngall, ngf,
    lsem, xs, xr, ws, wr, rss, rsr, ags, agr, gs, gr, fs, fr, zs, zr, z2s, z2r, osem, near, near_z, mid, far, held, hs, hr,
):
    nz = n_rep // 4
    tokens = ct.shape[0]
    pieces = [(sum(PIECES[:c]), size) for c, size in enumerate(PIECES)]
    block = w_hbm.shape[0]
    rep = lax.axis_index("rep")
    me = lax.axis_index("fsdp")
    y, x = me // NX, lax.rem(me, NX)
    core, z, ylo = lax.rem(rep, 2), lax.rem(rep // 2, nz), rep // (2 * nz)
    others = (2, 1, 3)

    def x_peer(o):
        return (rep, y * NX + lax.rem(x + o, NX))

    def z_peer(k):
        return (ylo * 2 * nz + lax.rem(z + k, nz) * 2 + core, me)

    y_peer = (rep, (1 - y) * NX + x)
    core_peer = (rep + 1 - 2 * core, me)
    ylo_peer = ((1 - ylo) * 2 * nz + z * 2 + core, me)

    def remote(src, dst, send, recv, device):
        return pltpu.make_async_remote_copy(
            src_ref=src, dst_ref=dst, send_sem=send, recv_sem=recv,
            device_id=device, device_id_type=MESH,
        )

    def columns(h):
        return pl.ds(h * HEAD, HEAD)

    loads = [
        pltpu.make_async_copy(w_hbm, wall.at[y], lsem.at[0]),
        pltpu.make_async_copy(ct_hbm, ct, lsem.at[1]),
        pltpu.make_async_copy(m_hbm, mv, lsem.at[2]),
        pltpu.make_async_copy(v_hbm, vv, lsem.at[3]),
    ]
    for yy in range(NY):
        start = pl.multiple_of((yy * NX + x) * block, block)
        loads.append(
            pltpu.make_async_copy(
                x_hbm.at[:, pl.ds(start, block)], xall.at[yy, pl.ds(0, tokens)], lsem.at[4 + yy]
            )
        )
    loads += [
        pltpu.make_async_copy(frag_hbm, frag_ref, lsem.at[6]),
        pltpu.make_async_copy(step_hbm, step_ref, lsem.at[7]),
        pltpu.make_async_copy(gf_hbm, gf_ref, lsem.at[8]),
        pltpu.make_async_copy(om_hbm, om_ref, lsem.at[9]),
    ]
    for load in loads:
        load.start()

    def y_near(step):
        place = lax.rem(NY * y + ylo + step, 4)
        return (lax.rem(place, 2) * 2 * nz + z * 2 + core, place // 2 * NX + x)

    def x_send(c, o):
        first, size = pieces[c]
        for yy in range(NY):
            start = pl.multiple_of((yy * NX + lax.rem(x + o, NX)) * block, block)
            x_copy[o, c, yy] = remote(
                x_hbm.at[pl.ds(first, size), pl.ds(start, block)],
                xall.at[yy, pl.ds(o * tokens + first, size)],
                xs.at[o, c, yy], xr.at[o, c, yy], x_peer(o),
            )
            x_copy[o, c, yy].start()

    def tell(semaphore, devices):
        for device in devices:
            pl.semaphore_signal(semaphore, inc=1, device_id=device, device_id_type=MESH)

    around = [x_peer(1), x_peer(3), y_near(1), y_near(3)]
    barrier = pltpu.get_barrier_semaphore()
    tell(barrier, around + [core_peer])
    if nz > 1:
        z_near = [z_peer(1), z_peer(nz - 1)]

        @pl.when(z == 0)
        def _():
            pl.semaphore_wait(barrier, len(around) + 1)
            tell(barrier, z_near)

        @pl.when(z != 0)
        def _():
            @pl.when(z != nz - 1)
            def _():
                tell(barrier, z_near[:1])

            @pl.when(z != 1)
            def _():
                tell(barrier, z_near[1:])

            pl.semaphore_wait(barrier, len(around) + 3)

            @pl.when(z == nz - 1)
            def _():
                tell(barrier, z_near[:1])

            @pl.when(z == 1)
            def _():
                tell(barrier, z_near[1:])
    else:
        pl.semaphore_wait(barrier, len(around) + 1)
    tell(near, around)
    x_copy = {}
    x_send(0, 1)
    x_send(0, 3)
    if nz > 1:
        @pl.when(z != 0)
        def _():
            tell(near_z, z_near)

    pl.semaphore_wait(near, len(around))
    x_send(0, 2)
    w_copy = remote(w_hbm, wall.at[y], ws.at[0], wr.at[0], y_peer)
    w_copy.start()
    for c in range(1, len(pieces)):
        for o in others:
            x_send(c, o)

    loads[0].wait()
    loads[6].wait()
    chosen = [jnp.where(frag_ref[0] == h, 1.0, 0.0) for h in range(KVH)]
    picked = sum(chosen[h] * wall[y, :, columns(h)].astype(f32) for h in range(KVH))
    fbuf[...] = picked.reshape(fbuf.shape)
    core_copy = remote(fbuf.at[:, :, 1 - core], fcore, fs.at[0], fr.at[0], core_peer)
    core_copy.start()
    core_copy.wait_recv()
    s1[...] = fbuf[:, :, core] + fcore[...]
    ylo_copy = remote(s1.at[1 - ylo], fyl, fs.at[1], fr.at[1], ylo_peer)
    ylo_copy.start()
    if nz > 1:
        @pl.when(z == 0)
        def _():
            pl.semaphore_wait(barrier, 2)
            tell(near_z, z_near)

        pl.semaphore_wait(near_z, 2)
        tell(mid, [z_peer(2), z_peer(nz - 2)])
        pl.semaphore_wait(mid, 2)
        tell(far, [z_peer(k) for k in (3, 4, nz - 4, nz - 3)])
    ylo_copy.wait_recv()
    s2[...] = s1[ylo] + fyl[...]
    if nz > 1:
        pl.semaphore_wait(far, 4)

    def z_sum(k):
        return remote(s2.at[lax.rem(z + k, nz)], zrecv.at[k], zs.at[k], zr.at[k], z_peer(k))

    def z_gather(k):
        return remote(ngall.at[z], ngall.at[z], z2s.at[k], z2r.at[k], z_peer(k))

    def each_z(act):
        if nz > 1:
            lax.fori_loop(1, nz, lambda k, carry: (act(k), carry)[1], 0)

    each_z(lambda k: z_sum(k).start())

    rs_copy, ag_copy, g_copy = {}, {}, {}
    ylo_back = remote(ngall.at[z, ylo], ngall.at[z, ylo], fs.at[2], fr.at[2], ylo_peer)
    core_back = remote(ngall, ngf.at[:, :, core], fs.at[3], fr.at[3], core_peer)
    outs = [
        pltpu.make_async_copy(ng_ref, ng_hbm, lsem.at[10]),
        pltpu.make_async_copy(nm_ref, nm_hbm, lsem.at[11]),
    ]
    arrived = set()

    def partial_keys(c, pair):
        first, size = pieces[c]
        wide = pl.ds(pair * 2 * HEAD, 2 * HEAD)
        for o in (1, 3, 2, 0):
            if (c, o) not in arrived:
                arrived.add((c, o))
                for yy in range(NY):
                    if o:
                        x_copy[o, c, yy].wait_recv()
                    elif c == 0:
                        loads[4 + yy].wait()
            rows = pl.ds(o * tokens + first, size)
            part = jnp.dot(xall[0, rows, :], wall[0, :, wide], preferred_element_type=f32)
            part += jnp.dot(xall[1, rows, :], wall[1, :, wide], preferred_element_type=f32)
            for i in range(2):
                own = part[:, i * HEAD:(i + 1) * HEAD]
                if o == 0:
                    kown[2 * pair + i, pl.ds(first, size)] = own
                else:
                    psend[o, 2 * pair + i, pl.ds(first, size)] = own.astype(bf16)

    def send_partial(c, h):
        first, size = pieces[c]
        for o in others:
            at = (o, h, pl.ds(first, size))
            rs_copy[o, c, h] = remote(
                psend.at[at], precv.at[at], rss.at[o, c, h], rsr.at[o, c, h], x_peer(NX - o)
            )
            rs_copy[o, c, h].start()

    half = tokens // 2
    upper, lower = pl.ds(0, half), pl.ds(half, half)

    def relay_partial(h):
        for i, (o, rows) in enumerate(((1, upper), (3, lower))):
            relayed[i, h] = remote(
                psend.at[2, h, rows], held.at[i, h], hs.at[i, h], hr.at[i, h], x_peer(o)
            )
            relayed[i, h].start()
        for o, rows in ((3, lower), (1, upper)):
            rs_copy[o, 0, h] = remote(
                psend.at[o, h, rows], precv.at[o, h, rows], rss.at[o, 0, h], rsr.at[o, 0, h], x_peer(NX - o)
            )
            rs_copy[o, 0, h].start()

    def relay_sum(h):
        for i, (o, rows) in enumerate(((3, upper), (1, lower))):
            relayed[i, h].wait_recv()
            psend[o, h, rows] = (psend[o, h, rows].astype(f32) + held[i, h].astype(f32)).astype(bf16)
            relayed[2 + i, h] = remote(
                psend.at[o, h, rows], precv.at[o, h, rows], hs.at[2 + i, h], hr.at[2 + i, h], x_peer(NX - o)
            )
            relayed[2 + i, h].start()

    relayed = {}

    def key_gradient(c, h):
        first, size = pieces[c]
        rows = pl.ds(first, size)
        keys = kown[h, rows]
        for o in others:
            if (o, c, h) in rs_copy:
                rs_copy[o, c, h].wait_recv()
        if (2, h) in relayed:
            relayed[2, h].wait_recv()
            relayed[3, h].wait_recv()
        for o in others:
            if (o, c, h) in rs_copy:
                keys += precv[o, h, rows].astype(f32)
        scale = lax.rsqrt(jnp.mean(keys * keys, axis=-1, keepdims=True) + norm_epsilon)
        normed = keys * scale
        upstream = ct[rows, columns(h)].astype(f32)
        along = jnp.mean(upstream * normed, axis=-1, keepdims=True)
        kgall[h, rows, :] = (scale * (upstream - normed * along)).astype(bf16)
        for o in others:
            ag_copy[o, c, h] = remote(
                kgall.at[h, rows], kgall.at[h, pl.ds(o * tokens + first, size)],
                ags.at[o, c, h], agr.at[o, c, h], x_peer(o),
            )
            ag_copy[o, c, h].start()

    def turn():
        for yy in range(NY):
            for piece in range(xall.shape[1] // 256):
                rows = pl.ds(piece * 256, 256)
                xt[yy, :, rows] = xall[yy, rows, :].T

    def send_gradient(h):
        for c in range(len(pieces)):
            for o in others:
                ag_copy[o, c, h].wait_recv()
        gsend[h] = jnp.dot(xt[1 - y], kgall[h], preferred_element_type=f32).astype(bf16)
        g_copy[h] = remote(gsend.at[h], grecv.at[h], gs.at[h], gr.at[h], y_peer)
        g_copy[h].start()

    def own_gradient(h):
        gown[h] = jnp.dot(xt[y], kgall[h], preferred_element_type=f32)

    from_first = lax.rem(z + 2, nz)

    def outer_update(early):
        if nz > 1:
            pl.when(from_first < 5 if early else from_first >= 5)(outer_rows)
        elif early:
            outer_rows()

    def outer_rows():
        each_z(lambda k: z_sum(k).wait_recv())
        total = s2[z]
        if nz > 1:
            total += jnp.sum(zrecv[pl.ds(1, nz - 1)], axis=0)
        loads[8].wait()
        loads[9].wait()
        average = gf_ref[...] - total / n_rep
        momentum_full = outer_beta * om_ref[...].astype(f32) + average
        global_new = gf_ref[...] - outer_rate * (average + outer_beta * momentum_full)
        ngall[z, ylo] = global_new
        ylo_back.start()
        ng_ref[...] = global_new
        nm_ref[...] = momentum_full.astype(bf16)
        for copy in outs:
            copy.start()

    def gather_rows(early):
        def start():
            ylo_back.wait_recv()
            each_z(lambda k: z_gather(k).start())

        if nz > 1:
            pl.when(from_first < 5 if early else from_first >= 5)(start)
        elif early:
            start()

    def core_return():
        each_z(lambda k: z_gather(k).wait_recv())
        core_back.start()
        ngf[:, :, core] = ngall[...]

    def all_left():
        for copy in [w_copy, core_copy, ylo_copy, ylo_back]:
            copy.wait_send()
        for copies in (x_copy, rs_copy, ag_copy, relayed):
            for copy in copies.values():
                copy.wait_send()
        each_z(lambda k: z_sum(k).wait_send())
        each_z(lambda k: z_gather(k).wait_send())

    def adam(h):
        if h == 0:
            core_back.wait_recv()
            loads[2].wait()
            loads[3].wait()
        time = jnp.full((1, HEAD), step_ref[0].astype(f32), f32)
        first_unbias = 1.0 / (1.0 - jnp.exp(time * math.log(beta_first)))
        second_unbias = 1.0 / (1.0 - jnp.exp(time * math.log(beta_second)))
        position = sum(jnp.where(frag_ref[j] == h, float(j), 0.0) for j in range(KVH))
        rate = rate_unit * (1.0 + position)
        g_copy[h].wait_recv()
        grad = gown[h] + grecv[h].astype(f32)
        first = beta_first * mv[:, columns(h)].astype(f32) + (1.0 - beta_first) * grad
        second = beta_second * vv[:, columns(h)].astype(f32) + (1.0 - beta_second) * grad * grad
        weight = wall[y, :, columns(h)].astype(f32)
        updated = weight - rate * (
            first * first_unbias / (jnp.sqrt(second * second_unbias) + adam_epsilon)
            + weight_decay * weight
        )
        share = (1.0 - mix_share) * chosen[h]
        mixed = jnp.concatenate([ngf[:, i].reshape(block // 2, HEAD) for i in range(2)], axis=0)
        updated = (1.0 - share) * updated + share * mixed
        wout[h] = updated.astype(bf16)
        fout[h] = first.astype(bf16)
        sout[h] = second.astype(bf16)
        for i, (buf, out) in enumerate(((wout, nw_hbm), (fout, nf_hbm), (sout, ns_hbm))):
            copy = pltpu.make_async_copy(buf.at[h], out.at[:, columns(h)], osem.at[i, h])
            copy.start()
            outs.append(copy)

    w_copy.wait_recv()
    loads[1].wait()
    loads[7].wait()
    steps = {
        "P": partial_keys, "R": send_partial, "K": key_gradient, "XT": turn, "G": send_gradient, "M": own_gradient,
        "Z": outer_update, "B": gather_rows, "T": relay_partial, "F": relay_sum, "CB": core_return, "L": all_left, "A": adam,
    }
    for name in ORDER:
        if name in steps:
            steps[name]()
        else:
            steps[name[0]](*map(int, name[1:]))

    for copy in [core_back, *g_copy.values()]:
        copy.wait_send()
    for copy in outs:
        copy.wait()


def writer(*refs):
    sources, targets, held, sems = refs[:5], refs[5:10], refs[10:15], refs[15]
    loads = [pltpu.make_async_copy(a, b, sems.at[0, i]) for i, (a, b) in enumerate(zip(sources, held))]
    stores = [pltpu.make_async_copy(a, b, sems.at[1, i]) for i, (a, b) in enumerate(zip(held, targets))]
    for load in loads:
        load.start()
    for load, store in zip(loads, stores):
        load.wait()
        store.start()
    for store in stores:
        store.wait()


def solution(mesh):
    n_rep = mesh.shape["rep"]
    nz = n_rep // 4

    def local(weights, first, second, inputs, cotangent, global_frag, outer_momentum, fragment, inner_step):
        block, wide = weights.shape[1:]
        tokens, din = inputs.shape[1:]
        share = global_frag.shape[0]
        hbm = pl.BlockSpec(memory_space=pltpu.HBM)
        dma = pltpu.SemaphoreType.DMA
        results = pl.pallas_call(
            functools.partial(kernel, n_rep),
            out_shape=[jax.ShapeDtypeStruct((block, wide), bf16)] * 3
            + [
                jax.ShapeDtypeStruct(global_frag.shape, f32),
                jax.ShapeDtypeStruct(outer_momentum.shape, bf16),
            ],
            in_specs=[hbm] * 9,
            out_specs=[hbm] * 5,
            scratch_shapes=[
                pltpu.VMEM((NY, NX * tokens, block), bf16),
                pltpu.VMEM((NY, block, NX * tokens), bf16),
                pltpu.VMEM((NY, block, wide), bf16),
                pltpu.VMEM((block, wide), bf16),
                pltpu.VMEM((block, wide), bf16),
                pltpu.VMEM((tokens, wide), bf16),
                pltpu.VMEM((KVH, tokens, HEAD), f32),
                pltpu.VMEM((NX, KVH, tokens, HEAD), bf16),
                pltpu.VMEM((NX, KVH, tokens, HEAD), bf16),
                pltpu.VMEM((KVH, NX * tokens, HEAD), bf16),
                pltpu.VMEM((KVH, block, HEAD), bf16),
                pltpu.VMEM((KVH, block, HEAD), bf16),
                pltpu.VMEM((KVH, block, HEAD), f32),
                pltpu.VMEM((KVH, block, HEAD), bf16),
                pltpu.VMEM((KVH, block, HEAD), bf16),
                pltpu.VMEM((KVH, block, HEAD), bf16),
                pltpu.VMEM(global_frag.shape, f32),
                pltpu.VMEM(outer_momentum.shape, bf16),
                pltpu.VMEM(global_frag.shape, f32),
                pltpu.VMEM(outer_momentum.shape, bf16),
                pltpu.SMEM(fragment.shape, jnp.int32),
                pltpu.SMEM(inner_step.shape, jnp.int32),
                pltpu.VMEM((2, nz, 2, share, HEAD), f32),
                pltpu.VMEM((2, nz, share, HEAD), f32),
                pltpu.VMEM((2, nz, share, HEAD), f32),
                pltpu.VMEM((nz, share, HEAD), f32),
                pltpu.VMEM((nz, share, HEAD), f32),
                pltpu.VMEM((nz, share, HEAD), f32),
                pltpu.VMEM((nz, 2, share, HEAD), f32),
                pltpu.VMEM((nz, 2, 2, share, HEAD), f32),
                dma((12,)),
                dma((NX, len(PIECES), NY)), dma((NX, len(PIECES), NY)),
                dma((1,)), dma((1,)),
                dma((NX, len(PIECES), KVH)), dma((NX, len(PIECES), KVH)),
                dma((NX, len(PIECES), KVH)), dma((NX, len(PIECES), KVH)),
                dma((KVH,)), dma((KVH,)),
                dma((4,)), dma((4,)),
                dma((nz,)), dma((nz,)), dma((nz,)), dma((nz,)),
                dma((3, KVH)),
                *[pltpu.SemaphoreType.REGULAR] * 4,
                pltpu.VMEM((2, KVH, tokens // 2, HEAD), bf16),
                dma((4, KVH)), dma((4, KVH)),
            ],
            compiler_params=pltpu.CompilerParams(
                collective_id=0, has_side_effects=True, vmem_limit_bytes=60 * 2**20
            ),
        )(
            inputs[0], weights[0], first[0], second[0], cotangent[0],
            global_frag, outer_momentum, fragment, inner_step,
        )
        results = pl.pallas_call(
            writer,
            out_shape=[jax.ShapeDtypeStruct(r.shape, r.dtype) for r in results],
            in_specs=[hbm] * 5,
            out_specs=[hbm] * 5,
            scratch_shapes=[*[pltpu.VMEM(r.shape, r.dtype) for r in results], dma((2, 5))],
            compiler_params=pltpu.CompilerParams(vmem_limit_bytes=60 * 2**20),
        )(*results)
        return (results[0][None], results[1][None], results[2][None], results[3], results[4])

    in_specs = (P("rep", "fsdp", None),) * 5 + (P(("fsdp", "rep"), None),) * 2 + (P(), P("rep"))
    out_specs = (P("rep", "fsdp", None),) * 3 + (P(("fsdp", "rep"), None),) * 2
    return jax.shard_map(local, mesh=mesh, in_specs=in_specs, out_specs=out_specs, check_vma=False)
```

```python
import functools
import math

import jax
import jax.numpy as jnp
from jax import lax
from jax.experimental import pallas as pl
from jax.experimental.pallas import tpu as pltpu
from jax.sharding import PartitionSpec as P

KVH = 4
HEAD = 128
NX = 4
NY = 2

beta_first = 0.9
beta_second = 0.95
rate_unit = 0.05
weight_decay = 0.1
adam_epsilon = 1e-08
norm_epsilon = 1e-06
outer_rate = 0.7
outer_beta = 0.9
mix_share = 0.5

PIECES = (192,)
ORDER = (
    "P00", "R00", "T1", "P01", "T2", "T3", "Z0", "XT", "K00", "F1", "F2", "F3", "B0", "K01", "Z1", "K02",
    "K03", "B1", "G0", "G1", "G2", "G3", "M0", "M1", "CB", "M2", "M3", "L", "A0", "A1", "A2", "A3",
)
MESH = pl.DeviceIdType.MESH
f32 = jnp.float32
bf16 = jnp.bfloat16


def kernel(
    n_rep,
    x_hbm, w_hbm, m_hbm, v_hbm, ct_hbm, gf_hbm, om_hbm, frag_hbm, step_hbm,
    nw_hbm, nf_hbm, ns_hbm, ng_hbm, nm_hbm,
    xall, xt, wall, mv, vv, ct, kown, psend, precv, kgall, gsend, grecv, gown, wout, fout, sout,
    gf_ref, om_ref, ng_ref, nm_ref, frag_ref, step_ref, fbuf, fcore, s1, fyl, s2, zrecv, ngall, ngf,
    lsem, xs, xr, ws, wr, rss, rsr, ags, agr, gs, gr, fs, fr, zs, zr, z2s, z2r, osem, near, near_z, mid, far, held, hs, hr,
):
    nz = n_rep // 4
    tokens = ct.shape[0]
    pieces = [(sum(PIECES[:c]), size) for c, size in enumerate(PIECES)]
    block = w_hbm.shape[0]
    rep = lax.axis_index("rep")
    me = lax.axis_index("fsdp")
    y, x = me // NX, lax.rem(me, NX)
    core, z, ylo = lax.rem(rep, 2), lax.rem(rep // 2, nz), rep // (2 * nz)
    others = (2, 1, 3)

    def x_peer(o):
        return (rep, y * NX + lax.rem(x + o, NX))

    def z_peer(k):
        return (ylo * 2 * nz + lax.rem(z + k, nz) * 2 + core, me)

    y_peer = (rep, (1 - y) * NX + x)
    core_peer = (rep + 1 - 2 * core, me)
    ylo_peer = ((1 - ylo) * 2 * nz + z * 2 + core, me)

    def remote(src, dst, send, recv, device):
        return pltpu.make_async_remote_copy(
            src_ref=src, dst_ref=dst, send_sem=send, recv_sem=recv,
            device_id=device, device_id_type=MESH,
        )

    def columns(h):
        return pl.ds(h * HEAD, HEAD)

    loads = [
        pltpu.make_async_copy(w_hbm, wall.at[y], lsem.at[0]),
        pltpu.make_async_copy(ct_hbm, ct, lsem.at[1]),
        pltpu.make_async_copy(m_hbm, mv, lsem.at[2]),
        pltpu.make_async_copy(v_hbm, vv, lsem.at[3]),
    ]
    for yy in range(NY):
        start = pl.multiple_of((yy * NX + x) * block, block)
        loads.append(
            pltpu.make_async_copy(
                x_hbm.at[:, pl.ds(start, block)], xall.at[yy, pl.ds(0, tokens)], lsem.at[4 + yy]
            )
        )
    loads += [
        pltpu.make_async_copy(frag_hbm, frag_ref, lsem.at[6]),
        pltpu.make_async_copy(step_hbm, step_ref, lsem.at[7]),
        pltpu.make_async_copy(gf_hbm, gf_ref, lsem.at[8]),
        pltpu.make_async_copy(om_hbm, om_ref, lsem.at[9]),
    ]
    for load in loads:
        load.start()

    def y_near(step):
        place = lax.rem(NY * y + ylo + step, 4)
        return (lax.rem(place, 2) * 2 * nz + z * 2 + core, place // 2 * NX + x)

    def x_send(c, o):
        first, size = pieces[c]
        for yy in range(NY):
            start = pl.multiple_of((yy * NX + lax.rem(x + o, NX)) * block, block)
            x_copy[o, c, yy] = remote(
                x_hbm.at[pl.ds(first, size), pl.ds(start, block)],
                xall.at[yy, pl.ds(o * tokens + first, size)],
                xs.at[o, c, yy], xr.at[o, c, yy], x_peer(o),
            )
            x_copy[o, c, yy].start()

    def tell(semaphore, devices):
        for device in devices:
            pl.semaphore_signal(semaphore, inc=1, device_id=device, device_id_type=MESH)

    around = [x_peer(1), x_peer(3), y_near(1), y_near(3)]
    barrier = pltpu.get_barrier_semaphore()
    tell(barrier, around + [core_peer])
    if nz > 1:
        z_near = [z_peer(1), z_peer(nz - 1)]

        @pl.when(z == 0)
        def _():
            pl.semaphore_wait(barrier, len(around) + 1)
            tell(barrier, z_near)

        @pl.when(z != 0)
        def _():
            @pl.when(z != nz - 1)
            def _():
                tell(barrier, z_near[:1])

            @pl.when(z != 1)
            def _():
                tell(barrier, z_near[1:])

            pl.semaphore_wait(barrier, len(around) + 3)

            @pl.when(z == nz - 1)
            def _():
                tell(barrier, z_near[:1])

            @pl.when(z == 1)
            def _():
                tell(barrier, z_near[1:])
    else:
        pl.semaphore_wait(barrier, len(around) + 1)
    tell(near, around)
    x_copy = {}
    x_send(0, 1)
    x_send(0, 3)
    if nz > 1:
        @pl.when(z != 0)
        def _():
            tell(near_z, z_near)

    pl.semaphore_wait(near, len(around))
    x_send(0, 2)
    w_copy = remote(w_hbm, wall.at[y], ws.at[0], wr.at[0], y_peer)
    w_copy.start()
    for c in range(1, len(pieces)):
        for o in others:
            x_send(c, o)

    loads[0].wait()
    loads[6].wait()
    chosen = [jnp.where(frag_ref[0] == h, 1.0, 0.0) for h in range(KVH)]
    picked = sum(chosen[h] * wall[y, :, columns(h)].astype(f32) for h in range(KVH))
    fbuf[...] = picked.reshape(fbuf.shape)
    core_copy = remote(fbuf.at[:, :, 1 - core], fcore, fs.at[0], fr.at[0], core_peer)
    core_copy.start()
    core_copy.wait_recv()
    s1[...] = fbuf[:, :, core] + fcore[...]
    ylo_copy = remote(s1.at[1 - ylo], fyl, fs.at[1], fr.at[1], ylo_peer)
    ylo_copy.start()
    if nz > 1:
        @pl.when(z == 0)
        def _():
            pl.semaphore_wait(barrier, 2)
            tell(near_z, z_near)

        pl.semaphore_wait(near_z, 2)
        tell(mid, [z_peer(2), z_peer(nz - 2)])
        pl.semaphore_wait(mid, 2)
        tell(far, [z_peer(k) for k in (3, 4, nz - 4, nz - 3)])
    ylo_copy.wait_recv()
    s2[...] = s1[ylo] + fyl[...]
    if nz > 1:
        pl.semaphore_wait(far, 4)

    def z_sum(k):
        return remote(s2.at[lax.rem(z + k, nz)], zrecv.at[k], zs.at[k], zr.at[k], z_peer(k))

    def z_gather(k):
        return remote(ngall.at[z], ngall.at[z], z2s.at[k], z2r.at[k], z_peer(k))

    def each_z(act):
        if nz > 1:
            lax.fori_loop(1, nz, lambda k, carry: (act(k), carry)[1], 0)

    each_z(lambda k: z_sum(k).start())

    rs_copy, ag_copy, g_copy = {}, {}, {}
    ylo_back = remote(ngall.at[z, ylo], ngall.at[z, ylo], fs.at[2], fr.at[2], ylo_peer)
    core_back = remote(ngall, ngf.at[:, :, core], fs.at[3], fr.at[3], core_peer)
    outs = [
        pltpu.make_async_copy(ng_ref, ng_hbm, lsem.at[10]),
        pltpu.make_async_copy(nm_ref, nm_hbm, lsem.at[11]),
    ]
    arrived = set()

    def partial_keys(c, pair):
        first, size = pieces[c]
        wide = pl.ds(pair * 2 * HEAD, 2 * HEAD)
        for o in (1, 3, 2, 0):
            if (c, o) not in arrived:
                arrived.add((c, o))
                for yy in range(NY):
                    if o:
                        x_copy[o, c, yy].wait_recv()
                    elif c == 0:
                        loads[4 + yy].wait()
            rows = pl.ds(o * tokens + first, size)
            part = jnp.dot(xall[0, rows, :], wall[0, :, wide], preferred_element_type=f32)
            part += jnp.dot(xall[1, rows, :], wall[1, :, wide], preferred_element_type=f32)
            for i in range(2):
                own = part[:, i * HEAD:(i + 1) * HEAD]
                if o == 0:
                    kown[2 * pair + i, pl.ds(first, size)] = own
                else:
                    psend[o, 2 * pair + i, pl.ds(first, size)] = own.astype(bf16)

    def send_partial(c, h):
        first, size = pieces[c]
        for o in others:
            at = (o, h, pl.ds(first, size))
            rs_copy[o, c, h] = remote(
                psend.at[at], precv.at[at], rss.at[o, c, h], rsr.at[o, c, h], x_peer(NX - o)
            )
            rs_copy[o, c, h].start()

    half = tokens // 2
    upper, lower = pl.ds(0, half), pl.ds(half, half)

    def relay_partial(h):
        for i, (o, rows) in enumerate(((1, upper), (3, lower))):
            relayed[i, h] = remote(
                psend.at[2, h, rows], held.at[i, h], hs.at[i, h], hr.at[i, h], x_peer(o)
            )
            relayed[i, h].start()
        for o, rows in ((3, lower), (1, upper)):
            rs_copy[o, 0, h] = remote(
                psend.at[o, h, rows], precv.at[o, h, rows], rss.at[o, 0, h], rsr.at[o, 0, h], x_peer(NX - o)
            )
            rs_copy[o, 0, h].start()

    def relay_sum(h):
        for i, (o, rows) in enumerate(((3, upper), (1, lower))):
            relayed[i, h].wait_recv()
            psend[o, h, rows] = (psend[o, h, rows].astype(f32) + held[i, h].astype(f32)).astype(bf16)
            relayed[2 + i, h] = remote(
                psend.at[o, h, rows], precv.at[o, h, rows], hs.at[2 + i, h], hr.at[2 + i, h], x_peer(NX - o)
            )
            relayed[2 + i, h].start()

    relayed = {}

    def key_gradient(c, h):
        first, size = pieces[c]
        rows = pl.ds(first, size)
        keys = kown[h, rows]
        for o in others:
            if (o, c, h) in rs_copy:
                rs_copy[o, c, h].wait_recv()
        if (2, h) in relayed:
            relayed[2, h].wait_recv()
            relayed[3, h].wait_recv()
        for o in others:
            if (o, c, h) in rs_copy:
                keys += precv[o, h, rows].astype(f32)
        scale = lax.rsqrt(jnp.mean(keys * keys, axis=-1, keepdims=True) + norm_epsilon)
        normed = keys * scale
        upstream = ct[rows, columns(h)].astype(f32)
        along = jnp.mean(upstream * normed, axis=-1, keepdims=True)
        kgall[h, rows, :] = (scale * (upstream - normed * along)).astype(bf16)
        for o in others:
            ag_copy[o, c, h] = remote(
                kgall.at[h, rows], kgall.at[h, pl.ds(o * tokens + first, size)],
                ags.at[o, c, h], agr.at[o, c, h], x_peer(o),
            )
            ag_copy[o, c, h].start()

    def turn():
        for yy in range(NY):
            for piece in range(xall.shape[1] // 256):
                rows = pl.ds(piece * 256, 256)
                xt[yy, :, rows] = xall[yy, rows, :].T

    def send_gradient(h):
        for c in range(len(pieces)):
            for o in others:
                ag_copy[o, c, h].wait_recv()
        gsend[h] = jnp.dot(xt[1 - y], kgall[h], preferred_element_type=f32).astype(bf16)
        g_copy[h] = remote(gsend.at[h], grecv.at[h], gs.at[h], gr.at[h], y_peer)
        g_copy[h].start()

    def own_gradient(h):
        gown[h] = jnp.dot(xt[y], kgall[h], preferred_element_type=f32)

    from_first = lax.rem(z + 2, nz)

    def outer_update(early):
        if nz > 1:
            pl.when(from_first < 5 if early else from_first >= 5)(outer_rows)
        elif early:
            outer_rows()

    def outer_rows():
        each_z(lambda k: z_sum(k).wait_recv())
        total = s2[z]
        if nz > 1:
            total += jnp.sum(zrecv[pl.ds(1, nz - 1)], axis=0)
        loads[8].wait()
        loads[9].wait()
        average = gf_ref[...] - total / n_rep
        momentum_full = outer_beta * om_ref[...].astype(f32) + average
        global_new = gf_ref[...] - outer_rate * (average + outer_beta * momentum_full)
        ngall[z, ylo] = global_new
        ylo_back.start()
        ng_ref[...] = global_new
        nm_ref[...] = momentum_full.astype(bf16)
        for copy in outs:
            copy.start()

    def gather_rows(early):
        def start():
            ylo_back.wait_recv()
            each_z(lambda k: z_gather(k).start())

        if nz > 1:
            pl.when(from_first < 5 if early else from_first >= 5)(start)
        elif early:
            start()

    def core_return():
        each_z(lambda k: z_gather(k).wait_recv())
        core_back.start()
        ngf[:, :, core] = ngall[...]

    def all_left():
        for copy in [w_copy, core_copy, ylo_copy, ylo_back]:
            copy.wait_send()
        for copies in (x_copy, rs_copy, ag_copy, relayed):
            for copy in copies.values():
                copy.wait_send()
        each_z(lambda k: z_sum(k).wait_send())
        each_z(lambda k: z_gather(k).wait_send())

    def adam(h):
        if h == 0:
            core_back.wait_recv()
            loads[2].wait()
            loads[3].wait()
        time = jnp.full((1, HEAD), step_ref[0].astype(f32), f32)
        first_unbias = 1.0 / (1.0 - jnp.exp(time * math.log(beta_first)))
        second_unbias = 1.0 / (1.0 - jnp.exp(time * math.log(beta_second)))
        position = sum(jnp.where(frag_ref[j] == h, float(j), 0.0) for j in range(KVH))
        rate = rate_unit * (1.0 + position)
        g_copy[h].wait_recv()
        grad = gown[h] + grecv[h].astype(f32)
        first = beta_first * mv[:, columns(h)].astype(f32) + (1.0 - beta_first) * grad
        second = beta_second * vv[:, columns(h)].astype(f32) + (1.0 - beta_second) * grad * grad
        weight = wall[y, :, columns(h)].astype(f32)
        updated = weight - rate * (
            first * first_unbias / (jnp.sqrt(second * second_unbias) + adam_epsilon)
            + weight_decay * weight
        )
        share = (1.0 - mix_share) * chosen[h]
        mixed = jnp.concatenate([ngf[:, i].reshape(block // 2, HEAD) for i in range(2)], axis=0)
        updated = (1.0 - share) * updated + share * mixed
        wout[h] = updated.astype(bf16)
        fout[h] = first.astype(bf16)
        sout[h] = second.astype(bf16)
        for i, (buf, out) in enumerate(((wout, nw_hbm), (fout, nf_hbm), (sout, ns_hbm))):
            copy = pltpu.make_async_copy(buf.at[h], out.at[:, columns(h)], osem.at[i, h])
            copy.start()
            outs.append(copy)

    w_copy.wait_recv()
    loads[1].wait()
    loads[7].wait()
    steps = {
        "P": partial_keys, "R": send_partial, "K": key_gradient, "XT": turn, "G": send_gradient, "M": own_gradient,
        "Z": outer_update, "B": gather_rows, "T": relay_partial, "F": relay_sum, "CB": core_return, "L": all_left, "A": adam,
    }
    for name in ORDER:
        if name in steps:
            steps[name]()
        else:
            steps[name[0]](*map(int, name[1:]))

    for copy in [core_back, *g_copy.values()]:
        copy.wait_send()
    for copy in outs:
        copy.wait()


def writer(*refs):
    sources, targets, held, sems = refs[:5], refs[5:10], refs[10:15], refs[15]
    loads = [pltpu.make_async_copy(a, b, sems.at[0, i]) for i, (a, b) in enumerate(zip(sources, held))]
    stores = [pltpu.make_async_copy(a, b, sems.at[1, i]) for i, (a, b) in enumerate(zip(held, targets))]
    for load in loads:
        load.start()
    for load, store in zip(loads, stores):
        load.wait()
        store.start()
    for store in stores:
        store.wait()


def solution(mesh):
    n_rep = mesh.shape["rep"]
    nz = n_rep // 4

    def local(weights, first, second, inputs, cotangent, global_frag, outer_momentum, fragment, inner_step):
        block, wide = weights.shape[1:]
        tokens, din = inputs.shape[1:]
        share = global_frag.shape[0]
        hbm = pl.BlockSpec(memory_space=pltpu.HBM)
        dma = pltpu.SemaphoreType.DMA
        results = pl.pallas_call(
            functools.partial(kernel, n_rep),
            out_shape=[jax.ShapeDtypeStruct((block, wide), bf16)] * 3
            + [
                jax.ShapeDtypeStruct(global_frag.shape, f32),
                jax.ShapeDtypeStruct(outer_momentum.shape, bf16),
            ],
            in_specs=[hbm] * 9,
            out_specs=[hbm] * 5,
            scratch_shapes=[
                pltpu.VMEM((NY, NX * tokens, block), bf16),
                pltpu.VMEM((NY, block, NX * tokens), bf16),
                pltpu.VMEM((NY, block, wide), bf16),
                pltpu.VMEM((block, wide), bf16),
                pltpu.VMEM((block, wide), bf16),
                pltpu.VMEM((tokens, wide), bf16),
                pltpu.VMEM((KVH, tokens, HEAD), f32),
                pltpu.VMEM((NX, KVH, tokens, HEAD), bf16),
                pltpu.VMEM((NX, KVH, tokens, HEAD), bf16),
                pltpu.VMEM((KVH, NX * tokens, HEAD), bf16),
                pltpu.VMEM((KVH, block, HEAD), bf16),
                pltpu.VMEM((KVH, block, HEAD), bf16),
                pltpu.VMEM((KVH, block, HEAD), f32),
                pltpu.VMEM((KVH, block, HEAD), bf16),
                pltpu.VMEM((KVH, block, HEAD), bf16),
                pltpu.VMEM((KVH, block, HEAD), bf16),
                pltpu.VMEM(global_frag.shape, f32),
                pltpu.VMEM(outer_momentum.shape, bf16),
                pltpu.VMEM(global_frag.shape, f32),
                pltpu.VMEM(outer_momentum.shape, bf16),
                pltpu.SMEM(fragment.shape, jnp.int32),
                pltpu.SMEM(inner_step.shape, jnp.int32),
                pltpu.VMEM((2, nz, 2, share, HEAD), f32),
                pltpu.VMEM((2, nz, share, HEAD), f32),
                pltpu.VMEM((2, nz, share, HEAD), f32),
                pltpu.VMEM((nz, share, HEAD), f32),
                pltpu.VMEM((nz, share, HEAD), f32),
                pltpu.VMEM((nz, share, HEAD), f32),
                pltpu.VMEM((nz, 2, share, HEAD), f32),
                pltpu.VMEM((nz, 2, 2, share, HEAD), f32),
                dma((12,)),
                dma((NX, len(PIECES), NY)), dma((NX, len(PIECES), NY)),
                dma((1,)), dma((1,)),
                dma((NX, len(PIECES), KVH)), dma((NX, len(PIECES), KVH)),
                dma((NX, len(PIECES), KVH)), dma((NX, len(PIECES), KVH)),
                dma((KVH,)), dma((KVH,)),
                dma((4,)), dma((4,)),
                dma((nz,)), dma((nz,)), dma((nz,)), dma((nz,)),
                dma((3, KVH)),
                *[pltpu.SemaphoreType.REGULAR] * 4,
                pltpu.VMEM((2, KVH, tokens // 2, HEAD), bf16),
                dma((4, KVH)), dma((4, KVH)),
            ],
            compiler_params=pltpu.CompilerParams(
                collective_id=0, has_side_effects=True, vmem_limit_bytes=60 * 2**20
            ),
        )(
            inputs[0], weights[0], first[0], second[0], cotangent[0],
            global_frag, outer_momentum, fragment, inner_step,
        )
        results = pl.pallas_call(
            writer,
            out_shape=[jax.ShapeDtypeStruct(r.shape, r.dtype) for r in results],
            in_specs=[hbm] * 5,
            out_specs=[hbm] * 5,
            scratch_shapes=[*[pltpu.VMEM(r.shape, r.dtype) for r in results], dma((2, 5))],
            compiler_params=pltpu.CompilerParams(vmem_limit_bytes=60 * 2**20),
        )(*results)
        return (results[0][None], results[1][None], results[2][None], results[3], results[4])

    in_specs = (P("rep", "fsdp", None),) * 5 + (P(("fsdp", "rep"), None),) * 2 + (P(), P("rep"))
    out_specs = (P("rep", "fsdp", None),) * 3 + (P(("fsdp", "rep"), None),) * 2
    return jax.shard_map(local, mesh=mesh, in_specs=in_specs, out_specs=out_specs, check_vma=False)
```

```python
import functools
import math

import jax
import jax.numpy as jnp
from jax import lax
from jax.experimental import pallas as pl
from jax.experimental.pallas import tpu as pltpu
from jax.sharding import PartitionSpec as P

KVH = 4
HEAD = 128
NX = 4
NY = 2

beta_first = 0.9
beta_second = 0.95
rate_unit = 0.05
weight_decay = 0.1
adam_epsilon = 1e-08
norm_epsilon = 1e-06
outer_rate = 0.7
outer_beta = 0.9
mix_share = 0.5

PIECES = (192,)
ORDER = (
    "P00", "R00", "T1", "P01", "T2", "T3", "Z0", "XT", "K00", "F1", "F2", "F3", "B0", "K01", "Z1", "K02",
    "K03", "B1", "G0", "G1", "G2", "G3", "M0", "M1", "M2", "M3", "L", "CB", "A0", "A1", "A2", "A3",
)
MESH = pl.DeviceIdType.MESH
f32 = jnp.float32
bf16 = jnp.bfloat16


def kernel(
    n_rep,
    x_hbm, w_hbm, m_hbm, v_hbm, ct_hbm, gf_hbm, om_hbm, frag_hbm, step_hbm,
    nw_hbm, nf_hbm, ns_hbm, ng_hbm, nm_hbm,
    xall, xt, wall, mv, vv, ct, kown, psend, precv, kgall, gsend, grecv, gown, wout, fout, sout,
    gf_ref, om_ref, ng_ref, nm_ref, frag_ref, step_ref, fbuf, fcore, s1, fyl, s2, zrecv, ngall, ngf,
    lsem, xs, xr, ws, wr, rss, rsr, ags, agr, gs, gr, fs, fr, zs, zr, z2s, z2r, osem, near, near_z, mid, far, held, hs, hr,
):
    nz = n_rep // 4
    tokens = ct.shape[0]
    pieces = [(sum(PIECES[:c]), size) for c, size in enumerate(PIECES)]
    block = w_hbm.shape[0]
    rep = lax.axis_index("rep")
    me = lax.axis_index("fsdp")
    y, x = me // NX, lax.rem(me, NX)
    core, z, ylo = lax.rem(rep, 2), lax.rem(rep // 2, nz), rep // (2 * nz)
    others = (2, 1, 3)

    def x_peer(o):
        return (rep, y * NX + lax.rem(x + o, NX))

    def z_peer(k):
        return (ylo * 2 * nz + lax.rem(z + k, nz) * 2 + core, me)

    y_peer = (rep, (1 - y) * NX + x)
    core_peer = (rep + 1 - 2 * core, me)
    ylo_peer = ((1 - ylo) * 2 * nz + z * 2 + core, me)

    def remote(src, dst, send, recv, device):
        return pltpu.make_async_remote_copy(
            src_ref=src, dst_ref=dst, send_sem=send, recv_sem=recv,
            device_id=device, device_id_type=MESH,
        )

    def columns(h):
        return pl.ds(h * HEAD, HEAD)

    loads = [
        pltpu.make_async_copy(w_hbm, wall.at[y], lsem.at[0]),
        pltpu.make_async_copy(ct_hbm, ct, lsem.at[1]),
        pltpu.make_async_copy(m_hbm, mv, lsem.at[2]),
        pltpu.make_async_copy(v_hbm, vv, lsem.at[3]),
    ]
    for yy in range(NY):
        start = pl.multiple_of((yy * NX + x) * block, block)
        loads.append(
            pltpu.make_async_copy(
                x_hbm.at[:, pl.ds(start, block)], xall.at[yy, pl.ds(0, tokens)], lsem.at[4 + yy]
            )
        )
    loads += [
        pltpu.make_async_copy(frag_hbm, frag_ref, lsem.at[6]),
        pltpu.make_async_copy(step_hbm, step_ref, lsem.at[7]),
        pltpu.make_async_copy(gf_hbm, gf_ref, lsem.at[8]),
        pltpu.make_async_copy(om_hbm, om_ref, lsem.at[9]),
    ]
    for load in loads:
        load.start()

    def y_near(step):
        place = lax.rem(NY * y + ylo + step, 4)
        return (lax.rem(place, 2) * 2 * nz + z * 2 + core, place // 2 * NX + x)

    def x_send(c, o):
        first, size = pieces[c]
        for yy in range(NY):
            start = pl.multiple_of((yy * NX + lax.rem(x + o, NX)) * block, block)
            x_copy[o, c, yy] = remote(
                x_hbm.at[pl.ds(first, size), pl.ds(start, block)],
                xall.at[yy, pl.ds(o * tokens + first, size)],
                xs.at[o, c, yy], xr.at[o, c, yy], x_peer(o),
            )
            x_copy[o, c, yy].start()

    def tell(semaphore, devices):
        for device in devices:
            pl.semaphore_signal(semaphore, inc=1, device_id=device, device_id_type=MESH)

    around = [x_peer(1), x_peer(3), y_near(1), y_near(3)]
    barrier = pltpu.get_barrier_semaphore()
    tell(barrier, around + [core_peer])
    if nz > 1:
        z_near = [z_peer(1), z_peer(nz - 1)]

        @pl.when(z == 0)
        def _():
            pl.semaphore_wait(barrier, len(around) + 1)
            tell(barrier, z_near)

        @pl.when(z != 0)
        def _():
            @pl.when(z != nz - 1)
            def _():
                tell(barrier, z_near[:1])

            @pl.when(z != 1)
            def _():
                tell(barrier, z_near[1:])

            pl.semaphore_wait(barrier, len(around) + 3)

            @pl.when(z == nz - 1)
            def _():
                tell(barrier, z_near[:1])

            @pl.when(z == 1)
            def _():
                tell(barrier, z_near[1:])
    else:
        pl.semaphore_wait(barrier, len(around) + 1)
    tell(near, around)
    x_copy = {}
    x_send(0, 1)
    x_send(0, 3)
    if nz > 1:
        @pl.when(z != 0)
        def _():
            tell(near_z, z_near)

    pl.semaphore_wait(near, len(around))
    x_send(0, 2)
    w_copy = remote(w_hbm, wall.at[y], ws.at[0], wr.at[0], y_peer)
    w_copy.start()
    for c in range(1, len(pieces)):
        for o in others:
            x_send(c, o)

    loads[0].wait()
    loads[6].wait()
    chosen = [jnp.where(frag_ref[0] == h, 1.0, 0.0) for h in range(KVH)]
    picked = sum(chosen[h] * wall[y, :, columns(h)].astype(f32) for h in range(KVH))
    fbuf[...] = picked.reshape(fbuf.shape)
    core_copy = remote(fbuf.at[:, :, 1 - core], fcore, fs.at[0], fr.at[0], core_peer)
    core_copy.start()
    core_copy.wait_recv()
    s1[...] = fbuf[:, :, core] + fcore[...]
    ylo_copy = remote(s1.at[1 - ylo], fyl, fs.at[1], fr.at[1], ylo_peer)
    ylo_copy.start()
    if nz > 1:
        @pl.when(z == 0)
        def _():
            pl.semaphore_wait(barrier, 2)
            tell(near_z, z_near)

        pl.semaphore_wait(near_z, 2)
        tell(mid, [z_peer(2), z_peer(nz - 2)])
        pl.semaphore_wait(mid, 2)
        tell(far, [z_peer(k) for k in (3, 4, nz - 4, nz - 3)])
    ylo_copy.wait_recv()
    s2[...] = s1[ylo] + fyl[...]
    if nz > 1:
        pl.semaphore_wait(far, 4)

    def z_sum(k):
        return remote(s2.at[lax.rem(z + k, nz)], zrecv.at[k], zs.at[k], zr.at[k], z_peer(k))

    def z_gather(k):
        return remote(ngall.at[z], ngall.at[z], z2s.at[k], z2r.at[k], z_peer(k))

    def each_z(act):
        if nz > 1:
            lax.fori_loop(1, nz, lambda k, carry: (act(k), carry)[1], 0)

    each_z(lambda k: z_sum(k).start())

    rs_copy, ag_copy, g_copy = {}, {}, {}
    ylo_back = remote(ngall.at[z, ylo], ngall.at[z, ylo], fs.at[2], fr.at[2], ylo_peer)
    core_back = remote(ngall, ngf.at[:, :, core], fs.at[3], fr.at[3], core_peer)
    outs = [
        pltpu.make_async_copy(ng_ref, ng_hbm, lsem.at[10]),
        pltpu.make_async_copy(nm_ref, nm_hbm, lsem.at[11]),
    ]
    arrived = set()

    def partial_keys(c, pair):
        first, size = pieces[c]
        wide = pl.ds(pair * 2 * HEAD, 2 * HEAD)
        for o in (1, 3, 2, 0):
            if (c, o) not in arrived:
                arrived.add((c, o))
                for yy in range(NY):
                    if o:
                        x_copy[o, c, yy].wait_recv()
                    elif c == 0:
                        loads[4 + yy].wait()
            rows = pl.ds(o * tokens + first, size)
            part = jnp.dot(xall[0, rows, :], wall[0, :, wide], preferred_element_type=f32)
            part += jnp.dot(xall[1, rows, :], wall[1, :, wide], preferred_element_type=f32)
            for i in range(2):
                own = part[:, i * HEAD:(i + 1) * HEAD]
                if o == 0:
                    kown[2 * pair + i, pl.ds(first, size)] = own
                else:
                    psend[o, 2 * pair + i, pl.ds(first, size)] = own.astype(bf16)

    def send_partial(c, h):
        first, size = pieces[c]
        for o in others:
            at = (o, h, pl.ds(first, size))
            rs_copy[o, c, h] = remote(
                psend.at[at], precv.at[at], rss.at[o, c, h], rsr.at[o, c, h], x_peer(NX - o)
            )
            rs_copy[o, c, h].start()

    half = tokens // 2
    upper, lower = pl.ds(0, half), pl.ds(half, half)

    def relay_partial(h):
        for i, (o, rows) in enumerate(((1, upper), (3, lower))):
            relayed[i, h] = remote(
                psend.at[2, h, rows], held.at[i, h], hs.at[i, h], hr.at[i, h], x_peer(o)
            )
            relayed[i, h].start()
        for o, rows in ((3, lower), (1, upper)):
            rs_copy[o, 0, h] = remote(
                psend.at[o, h, rows], precv.at[o, h, rows], rss.at[o, 0, h], rsr.at[o, 0, h], x_peer(NX - o)
            )
            rs_copy[o, 0, h].start()

    def relay_sum(h):
        for i, (o, rows) in enumerate(((3, upper), (1, lower))):
            relayed[i, h].wait_recv()
            psend[o, h, rows] = (psend[o, h, rows].astype(f32) + held[i, h].astype(f32)).astype(bf16)
            relayed[2 + i, h] = remote(
                psend.at[o, h, rows], precv.at[o, h, rows], hs.at[2 + i, h], hr.at[2 + i, h], x_peer(NX - o)
            )
            relayed[2 + i, h].start()

    relayed = {}

    def key_gradient(c, h):
        first, size = pieces[c]
        rows = pl.ds(first, size)
        keys = kown[h, rows]
        for o in others:
            if (o, c, h) in rs_copy:
                rs_copy[o, c, h].wait_recv()
        if (2, h) in relayed:
            relayed[2, h].wait_recv()
            relayed[3, h].wait_recv()
        for o in others:
            if (o, c, h) in rs_copy:
                keys += precv[o, h, rows].astype(f32)
        scale = lax.rsqrt(jnp.mean(keys * keys, axis=-1, keepdims=True) + norm_epsilon)
        normed = keys * scale
        upstream = ct[rows, columns(h)].astype(f32)
        along = jnp.mean(upstream * normed, axis=-1, keepdims=True)
        kgall[h, rows, :] = (scale * (upstream - normed * along)).astype(bf16)
        for o in others:
            ag_copy[o, c, h] = remote(
                kgall.at[h, rows], kgall.at[h, pl.ds(o * tokens + first, size)],
                ags.at[o, c, h], agr.at[o, c, h], x_peer(o),
            )
            ag_copy[o, c, h].start()

    def turn():
        for yy in range(NY):
            for piece in range(xall.shape[1] // 256):
                rows = pl.ds(piece * 256, 256)
                xt[yy, :, rows] = xall[yy, rows, :].T

    def send_gradient(h):
        for c in range(len(pieces)):
            for o in others:
                ag_copy[o, c, h].wait_recv()
        gsend[h] = jnp.dot(xt[1 - y], kgall[h], preferred_element_type=f32).astype(bf16)
        g_copy[h] = remote(gsend.at[h], grecv.at[h], gs.at[h], gr.at[h], y_peer)
        g_copy[h].start()

    def own_gradient(h):
        gown[h] = jnp.dot(xt[y], kgall[h], preferred_element_type=f32)

    from_first = lax.rem(z + 3, nz)

    def outer_update(early):
        if nz > 1:
            pl.when(from_first < 7 if early else from_first >= 7)(outer_rows)
        elif early:
            outer_rows()

    def outer_rows():
        each_z(lambda k: z_sum(k).wait_recv())
        total = s2[z]
        if nz > 1:
            total += jnp.sum(zrecv[pl.ds(1, nz - 1)], axis=0)
        loads[8].wait()
        loads[9].wait()
        average = gf_ref[...] - total / n_rep
        momentum_full = outer_beta * om_ref[...].astype(f32) + average
        global_new = gf_ref[...] - outer_rate * (average + outer_beta * momentum_full)
        ngall[z, ylo] = global_new
        ylo_back.start()
        ng_ref[...] = global_new
        nm_ref[...] = momentum_full.astype(bf16)
        for copy in outs:
            copy.start()

    def gather_rows(early):
        def start():
            ylo_back.wait_recv()
            each_z(lambda k: z_gather(k).start())

        if nz > 1:
            pl.when(from_first < 7 if early else from_first >= 7)(start)
        elif early:
            start()

    def core_return():
        each_z(lambda k: z_gather(k).wait_recv())
        core_back.start()
        ngf[:, :, core] = ngall[...]

    def all_left():
        for copy in [w_copy, core_copy, ylo_copy, ylo_back]:
            copy.wait_send()
        for copies in (x_copy, rs_copy, ag_copy, relayed):
            for copy in copies.values():
                copy.wait_send()
        each_z(lambda k: z_sum(k).wait_send())
        each_z(lambda k: z_gather(k).wait_send())

    def adam(h):
        if h == 0:
            core_back.wait_recv()
            loads[2].wait()
            loads[3].wait()
        time = jnp.full((1, HEAD), step_ref[0].astype(f32), f32)
        first_unbias = 1.0 / (1.0 - jnp.exp(time * math.log(beta_first)))
        second_unbias = 1.0 / (1.0 - jnp.exp(time * math.log(beta_second)))
        position = sum(jnp.where(frag_ref[j] == h, float(j), 0.0) for j in range(KVH))
        rate = rate_unit * (1.0 + position)
        g_copy[h].wait_recv()
        grad = gown[h] + grecv[h].astype(f32)
        first = beta_first * mv[:, columns(h)].astype(f32) + (1.0 - beta_first) * grad
        second = beta_second * vv[:, columns(h)].astype(f32) + (1.0 - beta_second) * grad * grad
        weight = wall[y, :, columns(h)].astype(f32)
        updated = weight - rate * (
            first * first_unbias / (jnp.sqrt(second * second_unbias) + adam_epsilon)
            + weight_decay * weight
        )
        share = (1.0 - mix_share) * chosen[h]
        mixed = jnp.concatenate([ngf[:, i].reshape(block // 2, HEAD) for i in range(2)], axis=0)
        updated = (1.0 - share) * updated + share * mixed
        wout[h] = updated.astype(bf16)
        fout[h] = first.astype(bf16)
        sout[h] = second.astype(bf16)
        for i, (buf, out) in enumerate(((wout, nw_hbm), (fout, nf_hbm), (sout, ns_hbm))):
            copy = pltpu.make_async_copy(buf.at[h], out.at[:, columns(h)], osem.at[i, h])
            copy.start()
            outs.append(copy)

    w_copy.wait_recv()
    loads[1].wait()
    loads[7].wait()
    steps = {
        "P": partial_keys, "R": send_partial, "K": key_gradient, "XT": turn, "G": send_gradient, "M": own_gradient,
        "Z": outer_update, "B": gather_rows, "T": relay_partial, "F": relay_sum, "CB": core_return, "L": all_left, "A": adam,
    }
    for name in ORDER:
        if name in steps:
            steps[name]()
        else:
            steps[name[0]](*map(int, name[1:]))

    for copy in [core_back, *g_copy.values()]:
        copy.wait_send()
    for copy in outs:
        copy.wait()


def writer(*refs):
    sources, targets, held, sems = refs[:5], refs[5:10], refs[10:15], refs[15]
    loads = [pltpu.make_async_copy(a, b, sems.at[0, i]) for i, (a, b) in enumerate(zip(sources, held))]
    stores = [pltpu.make_async_copy(a, b, sems.at[1, i]) for i, (a, b) in enumerate(zip(held, targets))]
    for load in loads:
        load.start()
    for load, store in zip(loads, stores):
        load.wait()
        store.start()
    for store in stores:
        store.wait()


def solution(mesh):
    n_rep = mesh.shape["rep"]
    nz = n_rep // 4

    def local(weights, first, second, inputs, cotangent, global_frag, outer_momentum, fragment, inner_step):
        block, wide = weights.shape[1:]
        tokens, din = inputs.shape[1:]
        share = global_frag.shape[0]
        hbm = pl.BlockSpec(memory_space=pltpu.HBM)
        dma = pltpu.SemaphoreType.DMA
        results = pl.pallas_call(
            functools.partial(kernel, n_rep),
            out_shape=[jax.ShapeDtypeStruct((block, wide), bf16)] * 3
            + [
                jax.ShapeDtypeStruct(global_frag.shape, f32),
                jax.ShapeDtypeStruct(outer_momentum.shape, bf16),
            ],
            in_specs=[hbm] * 9,
            out_specs=[hbm] * 5,
            scratch_shapes=[
                pltpu.VMEM((NY, NX * tokens, block), bf16),
                pltpu.VMEM((NY, block, NX * tokens), bf16),
                pltpu.VMEM((NY, block, wide), bf16),
                pltpu.VMEM((block, wide), bf16),
                pltpu.VMEM((block, wide), bf16),
                pltpu.VMEM((tokens, wide), bf16),
                pltpu.VMEM((KVH, tokens, HEAD), f32),
                pltpu.VMEM((NX, KVH, tokens, HEAD), bf16),
                pltpu.VMEM((NX, KVH, tokens, HEAD), bf16),
                pltpu.VMEM((KVH, NX * tokens, HEAD), bf16),
                pltpu.VMEM((KVH, block, HEAD), bf16),
                pltpu.VMEM((KVH, block, HEAD), bf16),
                pltpu.VMEM((KVH, block, HEAD), f32),
                pltpu.VMEM((KVH, block, HEAD), bf16),
                pltpu.VMEM((KVH, block, HEAD), bf16),
                pltpu.VMEM((KVH, block, HEAD), bf16),
                pltpu.VMEM(global_frag.shape, f32),
                pltpu.VMEM(outer_momentum.shape, bf16),
                pltpu.VMEM(global_frag.shape, f32),
                pltpu.VMEM(outer_momentum.shape, bf16),
                pltpu.SMEM(fragment.shape, jnp.int32),
                pltpu.SMEM(inner_step.shape, jnp.int32),
                pltpu.VMEM((2, nz, 2, share, HEAD), f32),
                pltpu.VMEM((2, nz, share, HEAD), f32),
                pltpu.VMEM((2, nz, share, HEAD), f32),
                pltpu.VMEM((nz, share, HEAD), f32),
                pltpu.VMEM((nz, share, HEAD), f32),
                pltpu.VMEM((nz, share, HEAD), f32),
                pltpu.VMEM((nz, 2, share, HEAD), f32),
                pltpu.VMEM((nz, 2, 2, share, HEAD), f32),
                dma((12,)),
                dma((NX, len(PIECES), NY)), dma((NX, len(PIECES), NY)),
                dma((1,)), dma((1,)),
                dma((NX, len(PIECES), KVH)), dma((NX, len(PIECES), KVH)),
                dma((NX, len(PIECES), KVH)), dma((NX, len(PIECES), KVH)),
                dma((KVH,)), dma((KVH,)),
                dma((4,)), dma((4,)),
                dma((nz,)), dma((nz,)), dma((nz,)), dma((nz,)),
                dma((3, KVH)),
                *[pltpu.SemaphoreType.REGULAR] * 4,
                pltpu.VMEM((2, KVH, tokens // 2, HEAD), bf16),
                dma((4, KVH)), dma((4, KVH)),
            ],
            compiler_params=pltpu.CompilerParams(
                collective_id=0, has_side_effects=True, vmem_limit_bytes=60 * 2**20
            ),
        )(
            inputs[0], weights[0], first[0], second[0], cotangent[0],
            global_frag, outer_momentum, fragment, inner_step,
        )
        results = pl.pallas_call(
            writer,
            out_shape=[jax.ShapeDtypeStruct(r.shape, r.dtype) for r in results],
            in_specs=[hbm] * 5,
            out_specs=[hbm] * 5,
            scratch_shapes=[*[pltpu.VMEM(r.shape, r.dtype) for r in results], dma((2, 5))],
            compiler_params=pltpu.CompilerParams(vmem_limit_bytes=60 * 2**20),
        )(*results)
        return (results[0][None], results[1][None], results[2][None], results[3], results[4])

    in_specs = (P("rep", "fsdp", None),) * 5 + (P(("fsdp", "rep"), None),) * 2 + (P(), P("rep"))
    out_specs = (P("rep", "fsdp", None),) * 3 + (P(("fsdp", "rep"), None),) * 2
    return jax.shard_map(local, mesh=mesh, in_specs=in_specs, out_specs=out_specs, check_vma=False)
```
